32 devices in a mesh: train: 8 (over z, y), dom: 4 (over x, core).
Axes of the slice: x: 2, y: 2, z: 4, core: 2. Of those that a mesh axis runs over, the one named last changes fastest.
Arguments:
- particles: float32 [4, 512, 4096], P(None, 'train', 'dom'), may hold values from -16 to 16
- slice_bin: int32 [512, 4096], P('train', 'dom'), may hold values from 0 to 127
- bunch_counts: int32 [512], P('train'), may hold values from 1365 to 4096, as said below
- past_moments: float32 [2, 512, 64], P(None, 'train'), may hold values from -6 to 6
- wake_lags: float32 [1535], replicated, may hold values from 0 to 2
- wake_matrix: float32 [64, 64], replicated, may hold values from -0.1875 to 0.1875
- adjust_phase: float32 [2], replicated, may hold values from -3.140625 to 3.140625
Outputs:
- tracked: float32 [4, 512, 4096], P(None, 'train', 'dom')
- moments_now: float32 [512, 64], P('train')
The draws below stay inside these ranges and needn't reach their ends.
Inputs may be any that keep to these rules, and one draw needn't show every extreme that they name: `bunch_counts`: some bunch holds exactly 4096 live macroparticles in every draw.
All inputs are finite; a program needn't handle non-finite values.
Results may differ from the reference program's by a relative error of at most 0.0003.
Values sent between devices are 32-bit elements; how exact they have to be, the bound alone decides.
A program may use at most 64 MiB of HBM per device.

```python
import jax
import jax.numpy as jnp
from jax import lax

K = 32
NBIN = 128
NB = 512
PART = 4096


def particle_fields(key):
    slice_values = jax.random.randint(jax.random.fold_in(key, 11), (NB, PART), 0, NBIN, dtype=jnp.int32)
    centers = 2.0 * (slice_values.astype(jnp.float32) + 0.5) / NBIN - 1.0
    mode_amps = jax.random.normal(jax.random.fold_in(key, 12), (2, NB, K), jnp.float32)
    jitter = jax.random.normal(jax.random.fold_in(key, 14), (4, NB, PART), jnp.float32)
    previous = jnp.ones_like(centers)
    current = centers
    pattern_x = mode_amps[0, :, 0:1] * previous + mode_amps[0, :, 1:2] * current
    pattern_y = mode_amps[1, :, 0:1] * previous + mode_amps[1, :, 1:2] * current
    for degree in range(1, K - 1):
        following = ((2 * degree + 1) * centers * current - degree * previous) / (degree + 1)
        pattern_x = pattern_x + mode_amps[0, :, degree + 1:degree + 2] * following
        pattern_y = pattern_y + mode_amps[1, :, degree + 1:degree + 2] * following
        previous = current
        current = following
    slot_ramp = 0.5 + 1.5 * jnp.arange(PART, dtype=jnp.float32)[None, :] / PART
    zero_field = jnp.zeros_like(centers)
    kick_fields_all = jitter + jnp.stack((pattern_x * slot_ramp, zero_field, pattern_y * slot_ramp, zero_field))
    return (slice_values, jnp.clip(kick_fields_all, -16.0, 16.0))


def draw_particles(key, part):
    return particle_fields(key)[1]


def draw_slice_bin(key, part):
    return particle_fields(key)[0]


def draw_bunch_counts(key, part):
    values = jax.random.randint(jax.random.fold_in(key, 21), (NB,), PART // 3, PART + 1, dtype=jnp.int32)
    fullest = jax.random.randint(jax.random.fold_in(key, 22), (), 0, NB, dtype=jnp.int32)
    return jnp.where(jnp.arange(NB, dtype=jnp.int32) == fullest, PART, values).astype(jnp.int32)


def draw_wake_lags(key, part):
    lag_values = jnp.arange(1, 3 * NB, dtype=jnp.int32).astype(jnp.float32)
    smooth_part = jax.lax.rsqrt(lag_values)
    rough = jnp.exp(jax.random.uniform(jax.random.fold_in(key, 32), (3 * NB - 1,), jnp.float32, -0.69, 0.69))
    return jnp.clip(smooth_part * rough, 0.0, 2.0)


def block_levels(rng, shape, split, least, top_value):
    level = 1.0
    for dim, parts in split:
        draws = jax.random.uniform(jax.random.fold_in(jax.random.fold_in(rng, 6), dim), (parts,), jnp.float32, least / len(split), top_value / len(split))
        level = level * jnp.repeat(jnp.exp(draws), shape[dim] // parts).reshape((-1,) + (1,) * (len(shape) - 1 - dim))
    return level


def bell_draw(rng, extent, width, most, shards=(), kind=jnp.bfloat16):
    array = width * jax.random.normal(rng, extent, jnp.float32)
    if shards:
        array = array * block_levels(rng, extent, shards, -0.22, 0.18)
    return jnp.clip(array, -most, most).astype(kind)


def setup_inputs(seed: int = 0) -> dict:
    seeds = jax.random.split(jax.random.key(seed), 8)
    return {
        "particles": draw_particles(jax.random.fold_in(seeds[7], 71), 0),
        "slice_bin": draw_slice_bin(jax.random.fold_in(seeds[7], 71), 0),
        "bunch_counts": draw_bunch_counts(jax.random.fold_in(seeds[7], 71), 0),
        "past_moments": bell_draw(seeds[3], (2, NB, 2 * K), 1.0, 6.0, ((1, 8),), jnp.float32),
        "wake_lags": draw_wake_lags(jax.random.fold_in(seeds[7], 71), 0),
        "wake_matrix": bell_draw(seeds[5], (2 * K, 2 * K), (32 * K) ** -0.5, 0.1875, (), jnp.float32),
        "adjust_phase": jnp.clip(jax.random.uniform(seeds[6], (2,), jnp.float32, -3.140625, 3.140625), -3.140625, 3.140625),
    }


def legendre_table(count_bins, orders):
    centers = 2.0 * (jnp.arange(count_bins, dtype=jnp.float32) + 0.5) / count_bins - 1.0
    columns = [jnp.ones_like(centers), centers]
    for degree in range(1, orders - 1):
        columns.append(((2 * degree + 1) * centers * columns[degree] - degree * columns[degree - 1]) / (degree + 1))
    return jnp.stack(columns[:orders], axis=1)


def wake_response_kernel(targets, source_first, number, turn_back, bunches_all, wake_lags):
    sources = source_first + jnp.arange(number, dtype=jnp.int32)
    lag_index = (targets[:, None] - sources[None, :] + turn_back * bunches_all).astype(jnp.int32)
    table_index = jnp.clip(lag_index - 1, 0, wake_lags.shape[0] - 1).astype(jnp.int32)
    values = jnp.take(wake_lags, table_index)
    return jnp.where(lag_index > 0, values, jnp.zeros_like(values))


def reference(particles, slice_bin, bunch_counts, past_moments, wake_lags, wake_matrix, adjust_phase):
    orders = wake_matrix.shape[0] // 2
    bunches_all = particles.shape[1]
    slot_total = particles.shape[2]
    legendre_basis = legendre_table(NBIN, orders)
    slot_index = jnp.arange(slot_total, dtype=jnp.int32)
    alive_particle_mask = (slot_index[None, :] < bunch_counts[:, None]).astype(jnp.float32)
    planes = jnp.stack((particles[0], particles[2])) * alive_particle_mask[None]
    segment_ids = (jnp.arange(bunches_all, dtype=jnp.int32)[:, None] * NBIN + slice_bin).reshape(-1)
    slice_binned = jnp.stack([jax.ops.segment_sum(planes[plane].reshape(-1), segment_ids, num_segments=bunches_all * NBIN) for plane in range(2)])
    slice_binned = slice_binned.reshape(2, bunches_all, NBIN)
    projected_moments = jnp.einsum("yaz,zu->ayu", slice_binned, legendre_basis, precision=lax.Precision.HIGHEST)
    degree_weight = (2 * jnp.arange(orders, dtype=jnp.int32) + 1).astype(jnp.float32)
    moments_now = (projected_moments * degree_weight[None, None, :] / bunch_counts.astype(jnp.float32)[:, None, None]).reshape(bunches_all, 2 * orders)
    targets = jnp.arange(bunches_all, dtype=jnp.int32)
    convolved = jnp.zeros((bunches_all, 2 * orders), jnp.float32)
    for turn_back, source in ((0, moments_now), (1, past_moments[0]), (2, past_moments[1])):
        kernel = wake_response_kernel(targets, 0, bunches_all, turn_back, bunches_all, wake_lags)
        convolved = convolved + jnp.dot(kernel, source, precision=lax.Precision.HIGHEST, preferred_element_type=jnp.float32)
    kick_modes = jnp.dot(convolved, wake_matrix, precision=lax.Precision.HIGHEST, preferred_element_type=jnp.float32)
    kick_table = jnp.einsum("bck,nk->bcn", kick_modes.reshape(bunches_all, 2, orders), legendre_basis, precision=lax.Precision.HIGHEST)
    kick_x = jnp.take_along_axis(kick_table[:, 0, :], slice_bin, axis=1)
    kick_y = jnp.take_along_axis(kick_table[:, 1, :], slice_bin, axis=1)
    cosine = jnp.cos(adjust_phase)
    sine_phase = jnp.sin(adjust_phase)
    tracked = jnp.stack((
        cosine[0] * particles[0] + sine_phase[0] * particles[1],
        -sine_phase[0] * particles[0] + cosine[0] * particles[1] + kick_x,
        cosine[1] * particles[2] + sine_phase[1] * particles[3],
        -sine_phase[1] * particles[2] + cosine[1] * particles[3] + kick_y))
    return tracked, moments_now
```

```python
import functools

import jax
import jax.numpy as jnp
import numpy as np
from jax import lax
from jax.experimental import pallas as pl
from jax.experimental.pallas import tpu as pltpu
from jax.sharding import PartitionSpec as P

NBIN = 128
LANES = 128
MESH = pl.DeviceIdType.MESH
F32 = jnp.float32
BF16 = jnp.bfloat16


def split(a):
    high = a.astype(BF16)
    return high, (a - high.astype(F32)).astype(BF16)


def dot(a, b):
    return jnp.dot(a, b, preferred_element_type=F32)


def dot3(a_parts, b_parts):
    (ah, al), (bh, bl) = a_parts, b_parts
    return dot(ah, bh) + (dot(ah, bl) + dot(al, bh))


def lane_iota(rows):
    return lax.broadcasted_iota(jnp.int32, (rows, LANES), 1)


def merge(a, b, distance):
    low = (lane_iota(a.shape[0]) & distance) == 0
    return jnp.where(low, a, b) + pltpu.roll(jnp.where(low, b, a), distance, 1)


def tile_sum(a):
    parts = [a[:, i : i + LANES] for i in range(0, a.shape[1], LANES)]
    while len(parts) > 1:
        parts = [p + q for p, q in zip(parts[::2], parts[1::2])] + parts[len(parts) & ~1 :]
    return parts[0]


def moments_kernel(
    sections, doms, orders,
    particles, bins, counts, past, lags, wake, phase,
    table_out, coef_out, moments_out,
    x_buf, y_buf, bin_buf, e_buf, basis_buf, count_buf,
    mine, now_buf, past_buf, dom_buf, conv_mine, conv_buf,
    load_sem, past_send, past_recv, now_send, now_recv, dom_send, dom_recv, conv_send, conv_recv,
):
    bunches = counts.shape[1]
    half = bunches // 2
    chunks = half // 8
    width = 2 * orders
    bunches_all = bunches * sections
    own = 2 * sections // doms
    t = lax.axis_index("train")
    d = lax.axis_index("dom")

    barrier = pltpu.get_barrier_semaphore()
    for o in range(1, sections):
        pl.semaphore_signal(
            barrier, inc=1, device_id=(lax.rem(t + o, sections), d), device_id_type=MESH
        )
    for o in range(1, doms):
        pl.semaphore_signal(
            barrier, inc=1, device_id=(t, lax.rem(d + o, doms)), device_id_type=MESH
        )
    loads = [
        pltpu.make_async_copy(particles.at[0], x_buf, load_sem.at[0]),
        pltpu.make_async_copy(particles.at[2], y_buf, load_sem.at[1]),
        pltpu.make_async_copy(bins, bin_buf, load_sem.at[2]),
    ]
    for copy in loads:
        copy.start()

    angle = phase[...]
    cosine, sine = jnp.cos(angle), jnp.sin(angle)
    for plane in range(2):
        coef_out[2 * plane : 2 * plane + 1, :] = jnp.broadcast_to(
            cosine[:, plane : plane + 1], (1, LANES)
        )
        coef_out[2 * plane + 1 : 2 * plane + 2, :] = jnp.broadcast_to(
            sine[:, plane : plane + 1], (1, LANES)
        )
    eye = lax.broadcasted_iota(jnp.int32, (bunches, bunches), 0) == lax.broadcasted_iota(
        jnp.int32, (bunches, bunches), 1
    )
    count_f = counts[...].astype(F32)
    column = jnp.sum(jnp.where(eye, count_f, 0.0), axis=1, keepdims=True)
    count_buf[...] = jnp.broadcast_to(column, (bunches, LANES))

    basis_buf[...] = jnp.zeros_like(basis_buf)
    centers = (lane_iota(1).astype(F32) + 0.5) * (2.0 / NBIN) - 1.0
    previous, current = jnp.ones_like(centers), centers
    for k in range(orders):
        basis_buf[k : k + 1, 0:LANES] = previous
        basis_buf[orders + k : orders + k + 1, LANES : 2 * LANES] = previous
        following = ((2 * k + 3) * centers * current - (k + 1) * previous) / (k + 2)
        previous, current = current, following
    to_kick = dot3(split(wake[...]), split(basis_buf[...]))
    to_kick = jnp.concatenate([to_kick, to_kick], axis=0)
    to_kick = split(to_kick)

    rows = bunches_all // 32
    pad = e_buf.shape[0] - rows
    count_lags = lags.shape[1]
    e_buf[...] = jnp.zeros_like(e_buf)
    for row in range(pl.cdiv(count_lags, LANES)):
        size = min(LANES, count_lags - row * LANES)
        e_buf[pad + row : pad + row + 1, 0:size] = lags[:, row * LANES : row * LANES + size]
    plain = e_buf[...]
    lane = lane_iota(plain.shape[0])
    turned = jnp.take_along_axis(plain, LANES - 1 - lane, axis=1, mode="promise_in_bounds")
    moved = pltpu.roll(turned, LANES // 2, 1)
    mixed = jnp.where(lane < LANES // 2, moved, pltpu.roll(moved, 1, 0))
    odd = lax.rem(t, 2)
    e_buf[...] = jnp.where(odd == 1, mixed, turned)
    first_row = pad + rows - 1 - bunches_all // 64 + (t + 1) // 2
    target = lax.broadcasted_iota(jnp.int32, (bunches, LANES), 0)
    source = lane_iota(bunches)

    def toeplitz(tile_first, tiles):
        def rolled(m):
            row = e_buf[pl.ds(first_row - m, 1), :]
            return pltpu.roll(
                jnp.broadcast_to(row, (bunches, LANES)), 0, 1, stride=1, stride_axis=0
            )

        turned_rows = [rolled(tile_first + m) for m in range(-1, tiles)]
        return jnp.concatenate(
            [
                jnp.where(source >= target, turned_rows[m + 1], turned_rows[m])
                for m in range(tiles)
            ],
            axis=1,
        )

    w_now = split(toeplitz(2 * bunches_all // LANES, bunches_all // LANES))
    past_tiles = own * bunches // LANES
    w_past = split(toeplitz(d * past_tiles, past_tiles))

    pl.semaphore_wait(barrier, sections - 1 + doms - 1)
    late = t // own == d
    owned = jnp.logical_or(late, (sections + t) // own == d)
    turn = jnp.where(late, 1, 0)
    slot = lax.rem(t, own)

    def past_copy(o):
        return pltpu.make_async_remote_copy(
            src_ref=past.at[turn], dst_ref=past_buf.at[slot],
            send_sem=past_send.at[o - 1], recv_sem=past_recv.at[slot],
            device_id=(lax.rem(t + o, sections), d), device_id_type=MESH,
        )

    @pl.when(owned)
    def _():
        for o in range(1, sections):
            past_copy(o).start()
        past_buf[slot] = past[turn]

    for copy in loads:
        copy.wait()
    slots = x_buf.shape[1]
    slot_index = d * slots + lax.broadcasted_iota(jnp.int32, (8, slots), 1)
    k_lane = lane_iota(8) % orders
    scale = jnp.ones((8, LANES), F32)
    lead = 1.0
    for k in range(1, orders):
        lead = lead * (2 * k - 1) / k
        scale = jnp.where(k_lane == k, np.float32((2 * k + 1) * lead), scale)
    low_half = lane_iota(8) < width

    def group_sums(first):
        here = pl.ds(first, 8)
        z = (bin_buf[here, :].astype(F32) + 0.5) * (2.0 / NBIN) - 1.0
        count = count_buf[here, 0:1].astype(jnp.int32)
        alive = slot_index < count
        vx = jnp.where(alive, x_buf[here, :], 0.0)
        vy = jnp.where(alive, y_buf[here, :], 0.0)
        stacks = ([], [])
        before, at = None, None
        for k in range(orders):
            if k == 0:
                terms = (vx, vy)
            else:
                if k == 1:
                    before, at = jnp.ones_like(z), z
                elif k == 2:
                    before, at = at, z * at - np.float32(1 / 3)
                else:
                    n = k - 1
                    before, at = at, z * at - np.float32(n * n / (4 * n * n - 1)) * before
                terms = (vx * at, vy * at)
            for stack, term in zip(stacks, terms):
                value, level = tile_sum(term), 1
                while stack and stack[-1][1] == level:
                    value = merge(stack.pop()[0], value, level)
                    level *= 2
                stack.append((value, level))
        return merge(stacks[0][0][0], stacks[1][0][0], orders)

    def now_copy(o, j):
        return pltpu.make_async_remote_copy(
            src_ref=mine.at[j], dst_ref=now_buf.at[t, j],
            send_sem=now_send.at[o - 1, j], recv_sem=now_recv.at[o - 1, j],
            device_id=(lax.rem(t + o, sections), d), device_id_type=MESH,
        )

    def dom_copy(o, j):
        return pltpu.make_async_remote_copy(
            src_ref=mine.at[j], dst_ref=dom_buf.at[d, j],
            send_sem=dom_send.at[o - 1, j], recv_sem=dom_recv.at[o - 1, j],
            device_id=(t, lax.rem(d + o, doms)), device_id_type=MESH,
        )

    def chunk(j, carry):
        first = pl.multiple_of(j * 8, 8)
        second = pl.multiple_of(j * 8 + half, 8)
        total = merge(group_sums(first), group_sums(second), width)
        divisor = jnp.where(
            low_half, count_buf[pl.ds(first, 8), :], count_buf[pl.ds(second, 8), :]
        )
        moments = total * scale / divisor
        mine[j] = moments
        for o in range(1, sections):
            now_copy(o, j).start()
        for o in range(1, doms):
            dom_copy(o, j).start()
        now_buf[t, j] = moments
        dom_buf[d, j] = moments
        return carry

    lax.fori_loop(0, chunks, chunk, 0)

    for s in range(own):
        @pl.when(lax.rem(d * own + s, sections) != t)
        def _():
            pltpu.make_async_remote_copy(
                src_ref=past.at[0], dst_ref=past_buf.at[s],
                send_sem=past_send.at[0], recv_sem=past_recv.at[s],
                device_id=(t, d), device_id_type=MESH,
            ).wait_recv()
    stored = past_buf[...].reshape(own * bunches, width)
    convolved = dot3(w_past, split(stored))

    for o in range(1, sections):
        for j in range(chunks):
            now_copy(o, j).wait_recv()
    gathered = now_buf[...].reshape(sections, half, LANES)
    lower = lane_iota(half)[None] < width
    spread = jnp.concatenate(
        [jnp.where(lower, gathered, 0.0), jnp.where(lower, 0.0, gathered)], axis=1
    ).reshape(bunches_all, LANES)
    both = dot3(w_now, split(spread))
    convolved = convolved + (both[:, :width] + both[:, width:])
    packed = jnp.concatenate([convolved[:half], convolved[half:]], axis=1)
    conv_mine[...] = packed

    def conv_copy(o):
        return pltpu.make_async_remote_copy(
            src_ref=conv_mine, dst_ref=conv_buf.at[d],
            send_sem=conv_send.at[o - 1], recv_sem=conv_recv.at[o - 1],
            device_id=(t, lax.rem(d + o, doms)), device_id_type=MESH,
        )

    for o in range(1, doms):
        conv_copy(o).start()
    conv_buf[d] = packed

    for o in range(1, doms):
        for j in range(chunks):
            dom_copy(o, j).wait_recv()
    summed = dom_buf[0]
    for i in range(1, doms):
        summed = summed + dom_buf[i]
    summed = summed.reshape(half, LANES)
    moments_out[0:half, :] = summed[:, :width]
    moments_out[half:bunches, :] = summed[:, width:]

    for o in range(1, doms):
        conv_copy(o).wait_recv()
    total = conv_buf[0]
    for i in range(1, doms):
        total = total + conv_buf[i]
    lower = lane_iota(half) < width
    total = jnp.concatenate([jnp.where(lower, total, 0.0), jnp.where(lower, 0.0, total)], axis=0)
    table_out[...] = dot3(split(total), to_kick)

    @pl.when(owned)
    def _():
        for o in range(1, sections):
            past_copy(o).wait_send()

    for o in range(1, sections):
        for j in range(chunks):
            now_copy(o, j).wait_send()
    for o in range(1, doms):
        for j in range(chunks):
            dom_copy(o, j).wait_send()
        conv_copy(o).wait_send()


def track_kernel(particles, bins, table, coef, moments, tracked, moments_out):
    rows, slots = bins.shape
    for plane in range(2):
        cosine = jnp.broadcast_to(coef[2 * plane : 2 * plane + 1, :], (rows, LANES))
        sine = jnp.broadcast_to(coef[2 * plane + 1 : 2 * plane + 2, :], (rows, LANES))
        kicks = table[:, plane * NBIN : (plane + 1) * NBIN]
        for first in range(0, slots, LANES):
            here = slice(first, first + LANES)
            place, momentum = particles[2 * plane, :, here], particles[2 * plane + 1, :, here]
            kick = jnp.take_along_axis(kicks, bins[:, here], axis=1, mode="promise_in_bounds")
            tracked[2 * plane, :, here] = cosine * place + sine * momentum
            tracked[2 * plane + 1, :, here] = cosine * momentum - sine * place + kick
    moments_out[...] = moments[...]


def local(sections, doms, particles, slice_bin, bunch_counts, past_moments, wake_lags, wake_matrix, adjust_phase):
    _, bunches, slots = particles.shape
    width = wake_matrix.shape[0]
    orders = width // 2
    half = bunches // 2
    chunks = half // 8
    bunches_all = bunches * sections
    own = 2 * sections // doms
    lag_rows = bunches_all // 32
    pad = pl.cdiv(bunches_all // 128, 8) * 8
    vmem = pl.BlockSpec(memory_space=pltpu.VMEM)
    hbm = pl.BlockSpec(memory_space=pl.ANY)
    dma = pltpu.SemaphoreType.DMA
    table, coef, moments = pl.pallas_call(
        functools.partial(moments_kernel, sections, doms, orders),
        out_shape=(
            jax.ShapeDtypeStruct((bunches, 2 * NBIN), F32),
            jax.ShapeDtypeStruct((4, LANES), F32),
            jax.ShapeDtypeStruct((bunches, width), F32),
        ),
        in_specs=[hbm, hbm, vmem, vmem, vmem, vmem, vmem],
        out_specs=(vmem, vmem, vmem),
        scratch_shapes=[
            pltpu.VMEM((bunches, slots), F32),
            pltpu.VMEM((bunches, slots), F32),
            pltpu.VMEM((bunches, slots), jnp.int32),
            pltpu.VMEM((pad + lag_rows, LANES), F32),
            pltpu.VMEM((width, 2 * NBIN), F32),
            pltpu.VMEM((bunches, LANES), F32),
            pltpu.VMEM((chunks, 8, LANES), F32),
            pltpu.VMEM((sections, chunks, 8, LANES), F32),
            pltpu.VMEM((own, bunches, width), F32),
            pltpu.VMEM((doms, chunks, 8, LANES), F32),
            pltpu.VMEM((half, LANES), F32),
            pltpu.VMEM((doms, half, LANES), F32),
            dma((3,)),
            dma((sections - 1,)),
            dma((own,)),
            dma((sections - 1, chunks)),
            dma((sections - 1, chunks)),
            dma((doms - 1, chunks)),
            dma((doms - 1, chunks)),
            dma((doms - 1,)),
            dma((doms - 1,)),
        ],
        compiler_params=pltpu.CompilerParams(
            collective_id=0, has_side_effects=True, vmem_limit_bytes=32 * 1024 * 1024
        ),
        name="moments",
    )(
        particles,
        slice_bin,
        bunch_counts.reshape(1, -1),
        past_moments,
        wake_lags.reshape(1, -1),
        wake_matrix,
        adjust_phase.reshape(1, -1),
    )
    block = 16
    return pl.pallas_call(
        track_kernel,
        grid=(bunches // block,),
        out_shape=(
            jax.ShapeDtypeStruct(particles.shape, F32),
            jax.ShapeDtypeStruct((bunches, width), F32),
        ),
        in_specs=[
            pl.BlockSpec((4, block, slots), lambda i: (0, i, 0)),
            pl.BlockSpec((block, slots), lambda i: (i, 0)),
            pl.BlockSpec((block, 2 * NBIN), lambda i: (i, 0)),
            pl.BlockSpec((4, LANES), lambda i: (0, 0)),
            pl.BlockSpec((bunches, width), lambda i: (0, 0)),
        ],
        out_specs=(
            pl.BlockSpec((4, block, slots), lambda i: (0, i, 0)),
            pl.BlockSpec((bunches, width), lambda i: (0, 0)),
        ),
        compiler_params=pltpu.CompilerParams(vmem_limit_bytes=32 * 1024 * 1024),
        name="track",
    )(particles, slice_bin, table, coef, moments)


def solution(mesh):
    in_specs = (
        P(None, "train", "dom"),
        P("train", "dom"),
        P("train"),
        P(None, "train", None),
        P(),
        P(),
        P(),
    )
    out_specs = (P(None, "train", "dom"), P("train", None))
    body = functools.partial(local, mesh.shape["train"], mesh.shape["dom"])
    return jax.shard_map(body, mesh=mesh, in_specs=in_specs, out_specs=out_specs, check_vma=False)
```

```python
import functools

import jax
import jax.numpy as jnp
import numpy as np
from jax import lax
from jax.experimental import pallas as pl
from jax.experimental.pallas import tpu as pltpu
from jax.sharding import PartitionSpec as P

NBIN = 128
LANES = 128
MESH = pl.DeviceIdType.MESH
F32 = jnp.float32
BF16 = jnp.bfloat16


def split(a):
    high = a.astype(BF16)
    return high, (a - high.astype(F32)).astype(BF16)


def dot(a, b):
    return jnp.dot(a, b, preferred_element_type=F32)


def dot3(a_parts, b_parts):
    (ah, al), (bh, bl) = a_parts, b_parts
    return dot(ah, bh) + (dot(ah, bl) + dot(al, bh))


def lane_iota(rows):
    return lax.broadcasted_iota(jnp.int32, (rows, LANES), 1)


def merge(a, b, distance):
    low = (lane_iota(a.shape[0]) & distance) == 0
    return jnp.where(low, a, b) + pltpu.roll(jnp.where(low, b, a), distance, 1)


def tile_sum(a):
    parts = [a[:, i : i + LANES] for i in range(0, a.shape[1], LANES)]
    while len(parts) > 1:
        parts = [p + q for p, q in zip(parts[::2], parts[1::2])] + parts[len(parts) & ~1 :]
    return parts[0]


def moments_kernel(
    sections, doms, orders,
    particles, bins, counts, past, lags, wake, phase,
    out,
    x_buf, y_buf, bin_buf, count_in, lag_in, wake_in, phase_in, e_buf, basis_buf, count_buf,
    now_buf, past_buf, dom_buf, conv_buf,
    load_sem, past_send, past_recv, pair_sem,
):
    bunches = counts.shape[1]
    half = bunches // 2
    chunks = half // 8
    width = 2 * orders
    bunches_all = bunches * sections
    own = 2 * sections // doms
    t = lax.axis_index("train")
    d = lax.axis_index("dom")
    now_send, now_recv, dom_send, dom_recv, conv_send, conv_recv = [pair_sem.at[i] for i in range(6)]

    barrier = pltpu.get_barrier_semaphore()
    for o in range(1, sections):
        pl.semaphore_signal(
            barrier, inc=1, device_id=(lax.rem(t + o, sections), d), device_id_type=MESH
        )
    for o in range(1, doms):
        pl.semaphore_signal(
            barrier, inc=1, device_id=(t, lax.rem(d + o, doms)), device_id_type=MESH
        )
    pairs = [
        (counts, count_in),
        (bins, bin_buf),
        (particles.at[0], x_buf),
        (particles.at[2], y_buf),
        (lags, lag_in),
        (wake, wake_in),
        (phase, phase_in),
    ]
    loads = [
        pltpu.make_async_copy(src, dst, load_sem.at[i]) for i, (src, dst) in enumerate(pairs)
    ]
    for copy in loads:
        copy.start()

    late = t // own == d
    owned = jnp.logical_or(late, (sections + t) // own == d)
    turn = jnp.where(late, 1, 0)
    slot = lax.rem(t, own)

    def past_copy(o):
        return pltpu.make_async_remote_copy(
            src_ref=past.at[turn], dst_ref=past_buf.at[slot],
            send_sem=past_send.at[o - 1], recv_sem=past_recv.at[slot],
            device_id=(lax.rem(t + o, sections), d), device_id_type=MESH,
        )

    def past_here():
        return pltpu.make_async_copy(past.at[turn], past_buf.at[slot], load_sem.at[len(pairs)])

    @pl.when(owned)
    def _():
        past_here().start()

    basis_buf[...] = jnp.zeros_like(basis_buf)
    centers = (lane_iota(1).astype(F32) + 0.5) * (2.0 / NBIN) - 1.0
    previous, current = jnp.ones_like(centers), centers
    for k in range(orders):
        basis_buf[k : k + 1, 0:LANES] = previous
        basis_buf[orders + k : orders + k + 1, LANES : 2 * LANES] = previous
        following = np.float32((2 * k + 3) / (k + 2)) * centers * current
        following = following - np.float32((k + 1) / (k + 2)) * previous
        previous, current = current, following

    loads[0].wait()
    eye = lax.broadcasted_iota(jnp.int32, (bunches, bunches), 0) == lax.broadcasted_iota(
        jnp.int32, (bunches, bunches), 1
    )
    count_f = count_in[...].astype(F32)
    column = jnp.sum(jnp.where(eye, count_f, 0.0), axis=1, keepdims=True)
    count_buf[...] = jnp.broadcast_to(column, (bunches, LANES))

    pl.semaphore_wait(barrier, sections - 1 + doms - 1)

    @pl.when(owned)
    def _():
        for o in range(1, sections):
            past_copy(o).start()

    for copy in loads[1:4]:
        copy.wait()
    slots = x_buf.shape[1]
    slot_index = d * slots + lax.broadcasted_iota(jnp.int32, (8, slots), 1)
    k_lane = lane_iota(8) % orders
    scale = jnp.ones((8, LANES), F32)
    lead = 1.0
    for k in range(1, orders):
        lead = lead * (2 * k - 1) / k
        scale = jnp.where(k_lane == k, np.float32((2 * k + 1) * lead), scale)
    low_half = lane_iota(8) < width

    def group_sums(first):
        here = pl.ds(first, 8)
        z = (bin_buf[here, :].astype(F32) + 0.5) * (2.0 / NBIN) - 1.0
        count = count_buf[here, 0:1].astype(jnp.int32)
        alive = slot_index < count
        vx = jnp.where(alive, x_buf[here, :], 0.0)
        vy = jnp.where(alive, y_buf[here, :], 0.0)
        stacks = ([], [])
        before, at = None, None
        for k in range(orders):
            if k == 0:
                terms = (vx, vy)
            else:
                if k == 1:
                    before, at = jnp.ones_like(z), z
                elif k == 2:
                    before, at = at, z * at - np.float32(1 / 3)
                else:
                    n = k - 1
                    before, at = at, z * at - np.float32(n * n / (4 * n * n - 1)) * before
                terms = (vx * at, vy * at)
            for stack, term in zip(stacks, terms):
                value, level = tile_sum(term), 1
                while stack and stack[-1][1] == level:
                    value = merge(stack.pop()[0], value, level)
                    level *= 2
                stack.append((value, level))
        return merge(stacks[0][0][0], stacks[1][0][0], orders)

    def chunk(j, carry):
        first = pl.multiple_of(j * 8, 8)
        second = pl.multiple_of(j * 8 + half, 8)
        total = merge(group_sums(first), group_sums(second), width)
        divisor = jnp.where(
            low_half, count_buf[pl.ds(first, 8), :], count_buf[pl.ds(second, 8), :]
        )
        moments = total * scale / divisor
        now_buf[t, j] = moments
        dom_buf[d, j] = moments
        for o in range(1, sections):
            pltpu.make_async_remote_copy(
                src_ref=now_buf.at[t, j], dst_ref=now_buf.at[t, j],
                send_sem=now_send, recv_sem=now_recv,
                device_id=(lax.rem(t + o, sections), d), device_id_type=MESH,
            ).start()
        return carry

    lax.fori_loop(0, chunks, chunk, 0)

    def dom_copies(ref, send_sem, recv_sem):
        for o in range(1, doms):
            pltpu.make_async_remote_copy(
                src_ref=ref.at[d], dst_ref=ref.at[d], send_sem=send_sem, recv_sem=recv_sem,
                device_id=(t, lax.rem(d + o, doms)), device_id_type=MESH,
            ).start()

    def whole(ref, send_sem, recv_sem):
        part = ref.at[pl.ds(0, ref.shape[0] - 1)]
        return pltpu.make_async_remote_copy(
            src_ref=part, dst_ref=part, send_sem=send_sem, recv_sem=recv_sem,
            device_id=(t, d), device_id_type=MESH,
        )

    dom_copies(dom_buf, dom_send, dom_recv)

    loads[4].wait()
    rows = bunches_all // 32
    pad = e_buf.shape[0] - rows
    count_lags = lag_in.shape[-1]
    e_buf[...] = jnp.zeros_like(e_buf)
    for row in range(pl.cdiv(count_lags, LANES)):
        size = min(LANES, count_lags - row * LANES)
        e_buf[pad + row : pad + row + 1, 0:size] = lag_in[pl.ds(row * LANES, size)].reshape(1, size)
    plain = e_buf[...]
    lane = lane_iota(plain.shape[0])
    turned = jnp.take_along_axis(plain, LANES - 1 - lane, axis=1, mode="promise_in_bounds")
    moved = pltpu.roll(turned, LANES // 2, 1)
    mixed = jnp.where(lane < LANES // 2, moved, pltpu.roll(moved, 1, 0))
    odd = lax.rem(t, 2)
    e_buf[...] = jnp.where(odd == 1, mixed, turned)
    first_row = pad + rows - 1 - bunches_all // 64 + (t + 1) // 2
    target = lax.broadcasted_iota(jnp.int32, (bunches, LANES), 0)
    source = lane_iota(bunches)

    def toeplitz(tile_first, tiles):
        def rolled(m):
            row = e_buf[pl.ds(first_row - m, 1), :]
            return pltpu.roll(
                jnp.broadcast_to(row, (bunches, LANES)), 0, 1, stride=1, stride_axis=0
            )

        turned_rows = [rolled(tile_first + m) for m in range(-1, tiles)]
        return jnp.concatenate(
            [
                jnp.where(source >= target, turned_rows[m + 1], turned_rows[m])
                for m in range(tiles)
            ],
            axis=1,
        )

    w_now = split(toeplitz(2 * bunches_all // LANES, bunches_all // LANES))
    past_tiles = own * bunches // LANES
    w_past = split(toeplitz(d * past_tiles, past_tiles))

    for s in range(own):
        @pl.when(lax.rem(d * own + s, sections) != t)
        def _():
            pltpu.make_async_remote_copy(
                src_ref=past.at[0], dst_ref=past_buf.at[s],
                send_sem=past_send.at[0], recv_sem=past_recv.at[s],
                device_id=(t, d), device_id_type=MESH,
            ).wait_recv()

    @pl.when(owned)
    def _():
        past_here().wait()

    stored = past_buf[...].reshape(own * bunches, width)
    convolved = dot3(w_past, split(stored))

    whole(now_buf, now_send, now_recv).wait_recv()
    gathered = now_buf[...].reshape(sections, half, LANES)
    lower = lane_iota(half)[None] < width
    spread = jnp.concatenate(
        [jnp.where(lower, gathered, 0.0), jnp.where(lower, 0.0, gathered)], axis=1
    ).reshape(bunches_all, LANES)
    both = dot3(w_now, split(spread))
    convolved = convolved + (both[:, :width] + both[:, width:])
    conv_buf[d] = jnp.concatenate([convolved[:half], convolved[half:]], axis=1)
    dom_copies(conv_buf, conv_send, conv_recv)

    for copy in loads[5:]:
        copy.wait()
    to_kick = dot3(split(wake_in[...]), split(basis_buf[...]))
    to_kick = jnp.concatenate([to_kick, to_kick], axis=0)
    to_kick = split(to_kick)
    angle = phase_in[...]
    cosine, sine = jnp.cos(angle), jnp.sin(angle)
    for plane in range(2):
        row = 2 * bunches + 2 * plane
        out[row : row + 1, :] = jnp.broadcast_to(cosine[:, plane : plane + 1], (1, 2 * NBIN))
        out[row + 1 : row + 2, :] = jnp.broadcast_to(sine[:, plane : plane + 1], (1, 2 * NBIN))
    dom_wait = whole(dom_buf, dom_send, dom_recv)
    dom_wait.wait_recv()
    summed = dom_buf[0]
    for i in range(1, doms):
        summed = summed + dom_buf[i]
    summed = summed.reshape(half, LANES)
    out[bunches : bunches + half, 0:width] = summed[:, :width]
    out[bunches + half : 2 * bunches, 0:width] = summed[:, width:]

    @pl.when(owned)
    def _():
        for o in range(1, sections):
            past_copy(o).wait_send()

    whole(now_buf, now_send, now_recv).wait_send()
    dom_wait.wait_send()

    conv_wait = whole(conv_buf, conv_send, conv_recv)
    conv_wait.wait_recv()
    total = conv_buf[0]
    for i in range(1, doms):
        total = total + conv_buf[i]
    lower = lane_iota(half) < width
    total = jnp.concatenate([jnp.where(lower, total, 0.0), jnp.where(lower, 0.0, total)], axis=0)
    out[0:bunches, :] = dot3(split(total), to_kick)
    conv_wait.wait_send()


def track_kernel(particles, bins, table, tracked, moments_out, result, moments, sems):
    bunches, slots = bins.shape
    block = 16
    moments[...] = table[bunches : 2 * bunches, 0 : moments.shape[1]]
    through = pltpu.make_async_copy(moments, moments_out, sems.at[bunches // block])
    through.start()
    copies = []
    for i in range(bunches // block):
        rows = slice(i * block, (i + 1) * block)
        for plane in range(2):
            row = 2 * bunches + 2 * plane
            cosine = jnp.broadcast_to(table[row : row + 1, 0:LANES], (block, LANES))
            sine = jnp.broadcast_to(table[row + 1 : row + 2, 0:LANES], (block, LANES))
            kicks = table[rows, plane * NBIN : (plane + 1) * NBIN]
            for first in range(0, slots, LANES):
                here = slice(first, first + LANES)
                place = particles[2 * plane, rows, here]
                momentum = particles[2 * plane + 1, rows, here]
                kick = jnp.take_along_axis(
                    kicks, bins[rows, here], axis=1, mode="promise_in_bounds"
                )
                result[2 * plane, rows, here] = cosine * place + sine * momentum
                result[2 * plane + 1, rows, here] = cosine * momentum - sine * place + kick
        copy = pltpu.make_async_copy(result.at[:, rows, :], tracked.at[:, rows, :], sems.at[i])
        copy.start()
        copies.append(copy)
    for copy in copies:
        copy.wait()
    through.wait()


def local(sections, doms, particles, slice_bin, bunch_counts, past_moments, wake_lags, wake_matrix, adjust_phase):
    _, bunches, slots = particles.shape
    width = wake_matrix.shape[0]
    orders = width // 2
    half = bunches // 2
    chunks = half // 8
    bunches_all = bunches * sections
    own = 2 * sections // doms
    lag_rows = bunches_all // 32
    pad = pl.cdiv(bunches_all // 128, 8) * 8
    vmem = pl.BlockSpec(memory_space=pltpu.VMEM)
    hbm = pl.BlockSpec(memory_space=pltpu.HBM)
    dma = pltpu.SemaphoreType.DMA
    table = pl.pallas_call(
        functools.partial(moments_kernel, sections, doms, orders),
        out_shape=jax.ShapeDtypeStruct((2 * bunches + 8, 2 * NBIN), F32),
        in_specs=[hbm] * 7,
        out_specs=vmem,
        scratch_shapes=[
            pltpu.VMEM((bunches, slots), F32),
            pltpu.VMEM((bunches, slots), F32),
            pltpu.VMEM((bunches, slots), jnp.int32),
            pltpu.VMEM((1, bunches), jnp.int32),
            pltpu.VMEM(wake_lags.shape, F32),
            pltpu.VMEM((width, width), F32),
            pltpu.VMEM((1, 2), F32),
            pltpu.VMEM((pad + lag_rows, LANES), F32),
            pltpu.VMEM((width, 2 * NBIN), F32),
            pltpu.VMEM((bunches, LANES), F32),
            pltpu.VMEM((sections, chunks, 8, LANES), F32),
            pltpu.VMEM((own, bunches, width), F32),
            pltpu.VMEM((doms, chunks, 8, LANES), F32),
            pltpu.VMEM((doms, half, LANES), F32),
            dma((8,)),
            dma((sections - 1,)),
            dma((own,)),
            dma((6,)),
        ],
        compiler_params=pltpu.CompilerParams(
            collective_id=0, has_side_effects=True, vmem_limit_bytes=56 * 1024 * 1024
        ),
        name="moments",
    )(
        particles,
        slice_bin,
        bunch_counts.reshape(1, -1),
        past_moments,
        wake_lags,
        wake_matrix,
        adjust_phase.reshape(1, -1),
    )
    return pl.pallas_call(
        track_kernel,
        out_shape=(
            jax.ShapeDtypeStruct(particles.shape, F32),
            jax.ShapeDtypeStruct((bunches, width), F32),
        ),
        in_specs=[vmem, vmem, vmem],
        out_specs=(hbm, hbm),
        scratch_shapes=[pltpu.VMEM(particles.shape, F32), pltpu.VMEM((bunches, width), F32), dma((bunches // 16 + 1,))],
        compiler_params=pltpu.CompilerParams(vmem_limit_bytes=16 * 1024 * 1024),
        name="track",
    )(particles, slice_bin, table)


def solution(mesh):
    in_specs = (
        P(None, "train", "dom"),
        P("train", "dom"),
        P("train"),
        P(None, "train", None),
        P(),
        P(),
        P(),
    )
    out_specs = (P(None, "train", "dom"), P("train", None))
    body = functools.partial(local, mesh.shape["train"], mesh.shape["dom"])
    return jax.shard_map(body, mesh=mesh, in_specs=in_specs, out_specs=out_specs, check_vma=False)
```

```python
import functools

import jax
import jax.numpy as jnp
import numpy as np
from jax import lax
from jax.experimental import pallas as pl
from jax.experimental.pallas import tpu as pltpu
from jax.sharding import PartitionSpec as P

NBIN = 128
LANES = 128
MESH = pl.DeviceIdType.MESH
F32 = jnp.float32
BF16 = jnp.bfloat16


def split(a):
    high = a.astype(BF16)
    return high, (a - high.astype(F32)).astype(BF16)


def dot(a, b):
    return jnp.dot(a, b, preferred_element_type=F32)


def dot3(a_parts, b_parts):
    (ah, al), (bh, bl) = a_parts, b_parts
    return dot(ah, bh) + (dot(ah, bl) + dot(al, bh))


def lane_iota(rows):
    return lax.broadcasted_iota(jnp.int32, (rows, LANES), 1)


def merge(a, b, distance):
    low = (lane_iota(a.shape[0]) & distance) == 0
    return jnp.where(low, a, b) + pltpu.roll(jnp.where(low, b, a), distance, 1)


def tile_sum(a):
    parts = [a[:, i : i + LANES] for i in range(0, a.shape[1], LANES)]
    while len(parts) > 1:
        parts = [p + q for p, q in zip(parts[::2], parts[1::2])] + parts[len(parts) & ~1 :]
    return parts[0]


def moments_kernel(
    sections, doms, orders,
    particles, bins, counts, past, lags, wake, phase,
    out,
    x_buf, y_buf, bin_buf, count_in, lag_in, wake_in, phase_in, e_buf, basis_buf, count_buf,
    now_buf, past_buf, dom_buf, conv_buf,
    load_sem, past_send, past_recv, pair_sem,
):
    bunches = counts.shape[1]
    half = bunches // 2
    chunks = half // 8
    width = 2 * orders
    bunches_all = bunches * sections
    own = 2 * sections // doms
    t = lax.axis_index("train")
    d = lax.axis_index("dom")
    now_send, now_recv, dom_send, dom_recv, conv_send, conv_recv = [pair_sem.at[i] for i in range(6)]

    barrier = pltpu.get_barrier_semaphore()
    for o in range(1, sections):
        pl.semaphore_signal(
            barrier, inc=1, device_id=(lax.rem(t + o, sections), d), device_id_type=MESH
        )
    for o in range(1, doms):
        pl.semaphore_signal(
            barrier, inc=1, device_id=(t, lax.rem(d + o, doms)), device_id_type=MESH
        )
    pairs = [
        (counts, count_in),
        (bins, bin_buf),
        (particles.at[0], x_buf),
        (particles.at[2], y_buf),
        (lags, lag_in),
        (wake, wake_in),
        (phase, phase_in),
    ]
    loads = [
        pltpu.make_async_copy(src, dst, load_sem.at[i]) for i, (src, dst) in enumerate(pairs)
    ]
    for copy in loads:
        copy.start()

    late = t // own == d
    owned = jnp.logical_or(late, (sections + t) // own == d)
    turn = jnp.where(late, 1, 0)
    slot = lax.rem(t, own)

    def past_copy(o):
        return pltpu.make_async_remote_copy(
            src_ref=past.at[turn], dst_ref=past_buf.at[slot],
            send_sem=past_send.at[o - 1], recv_sem=past_recv.at[slot],
            device_id=(lax.rem(t + o, sections), d), device_id_type=MESH,
        )

    def past_here():
        return pltpu.make_async_copy(past.at[turn], past_buf.at[slot], load_sem.at[len(pairs)])

    @pl.when(owned)
    def _():
        past_here().start()

    basis_buf[...] = jnp.zeros_like(basis_buf)
    centers = (lane_iota(1).astype(F32) + 0.5) * (2.0 / NBIN) - 1.0
    previous, current = jnp.ones_like(centers), centers
    for k in range(orders):
        basis_buf[k : k + 1, 0:LANES] = previous
        basis_buf[orders + k : orders + k + 1, LANES : 2 * LANES] = previous
        following = np.float32((2 * k + 3) / (k + 2)) * centers * current
        following = following - np.float32((k + 1) / (k + 2)) * previous
        previous, current = current, following

    loads[0].wait()
    eye = lax.broadcasted_iota(jnp.int32, (bunches, bunches), 0) == lax.broadcasted_iota(
        jnp.int32, (bunches, bunches), 1
    )
    count_f = count_in[...].astype(F32)
    column = jnp.sum(jnp.where(eye, count_f, 0.0), axis=1, keepdims=True)
    count_buf[...] = jnp.broadcast_to(column, (bunches, LANES))

    pl.semaphore_wait(barrier, sections - 1 + doms - 1)

    @pl.when(owned)
    def _():
        for o in range(1, sections):
            past_copy(o).start()

    for copy in loads[1:4]:
        copy.wait()
    slots = x_buf.shape[1]
    slot_index = d * slots + lax.broadcasted_iota(jnp.int32, (8, slots), 1)
    k_lane = lane_iota(8) % orders
    scale = jnp.ones((8, LANES), F32)
    for k in range(1, orders):
        scale = jnp.where(k_lane == k, np.float32(2 * k + 1), scale)
    low_half = lane_iota(8) < width

    def group_sums(first):
        here = pl.ds(first, 8)
        places = bin_buf[here, :]
        places = [places[:, i : i + LANES] for i in range(0, slots, LANES)]
        count = count_buf[here, 0:1].astype(jnp.int32)
        alive = slot_index < count
        vx = jnp.where(alive, x_buf[here, :], 0.0)
        vy = jnp.where(alive, y_buf[here, :], 0.0)
        stacks = ([], [])
        for k in range(orders):
            if k == 0:
                terms = (vx, vy)
            else:
                row = jnp.broadcast_to(basis_buf[k : k + 1, 0:LANES], (8, LANES))
                at = jnp.concatenate(
                    [
                        jnp.take_along_axis(row, place, axis=1, mode="promise_in_bounds")
                        for place in places
                    ],
                    axis=1,
                )
                terms = (vx * at, vy * at)
            for stack, term in zip(stacks, terms):
                value, level = tile_sum(term), 1
                while stack and stack[-1][1] == level:
                    value = merge(stack.pop()[0], value, level)
                    level *= 2
                stack.append((value, level))
        return merge(stacks[0][0][0], stacks[1][0][0], orders)

    def chunk(j, carry):
        first = pl.multiple_of(j * 8, 8)
        second = pl.multiple_of(j * 8 + half, 8)
        total = merge(group_sums(first), group_sums(second), width)
        divisor = jnp.where(
            low_half, count_buf[pl.ds(first, 8), :], count_buf[pl.ds(second, 8), :]
        )
        moments = total * scale / divisor
        now_buf[t, j] = moments
        dom_buf[d, j] = moments
        for o in range(1, sections):
            pltpu.make_async_remote_copy(
                src_ref=now_buf.at[t, j], dst_ref=now_buf.at[t, j],
                send_sem=now_send, recv_sem=now_recv,
                device_id=(lax.rem(t + o, sections), d), device_id_type=MESH,
            ).start()
        return carry

    lax.fori_loop(0, chunks, chunk, 0)

    def dom_copies(ref, send_sem, recv_sem):
        for o in range(1, doms):
            pltpu.make_async_remote_copy(
                src_ref=ref.at[d], dst_ref=ref.at[d], send_sem=send_sem, recv_sem=recv_sem,
                device_id=(t, lax.rem(d + o, doms)), device_id_type=MESH,
            ).start()

    def whole(ref, send_sem, recv_sem):
        part = ref.at[pl.ds(0, ref.shape[0] - 1)]
        return pltpu.make_async_remote_copy(
            src_ref=part, dst_ref=part, send_sem=send_sem, recv_sem=recv_sem,
            device_id=(t, d), device_id_type=MESH,
        )

    dom_copies(dom_buf, dom_send, dom_recv)

    loads[4].wait()
    rows = bunches_all // 32
    pad = e_buf.shape[0] - rows
    count_lags = lag_in.shape[-1]
    e_buf[...] = jnp.zeros_like(e_buf)
    for row in range(pl.cdiv(count_lags, LANES)):
        size = min(LANES, count_lags - row * LANES)
        e_buf[pad + row : pad + row + 1, 0:size] = lag_in[pl.ds(row * LANES, size)].reshape(1, size)
    plain = e_buf[...]
    lane = lane_iota(plain.shape[0])
    turned = jnp.take_along_axis(plain, LANES - 1 - lane, axis=1, mode="promise_in_bounds")
    moved = pltpu.roll(turned, LANES // 2, 1)
    mixed = jnp.where(lane < LANES // 2, moved, pltpu.roll(moved, 1, 0))
    odd = lax.rem(t, 2)
    e_buf[...] = jnp.where(odd == 1, mixed, turned)
    first_row = pad + rows - 1 - bunches_all // 64 + (t + 1) // 2
    target = lax.broadcasted_iota(jnp.int32, (bunches, LANES), 0)
    source = lane_iota(bunches)

    def toeplitz(tile_first, tiles):
        def rolled(m):
            row = e_buf[pl.ds(first_row - m, 1), :]
            return pltpu.roll(
                jnp.broadcast_to(row, (bunches, LANES)), 0, 1, stride=1, stride_axis=0
            )

        turned_rows = [rolled(tile_first + m) for m in range(-1, tiles)]
        return jnp.concatenate(
            [
                jnp.where(source >= target, turned_rows[m + 1], turned_rows[m])
                for m in range(tiles)
            ],
            axis=1,
        )

    w_now = split(toeplitz(2 * bunches_all // LANES, bunches_all // LANES))
    past_tiles = own * bunches // LANES
    w_past = split(toeplitz(d * past_tiles, past_tiles))

    for s in range(own):
        @pl.when(lax.rem(d * own + s, sections) != t)
        def _():
            pltpu.make_async_remote_copy(
                src_ref=past.at[0], dst_ref=past_buf.at[s],
                send_sem=past_send.at[0], recv_sem=past_recv.at[s],
                device_id=(t, d), device_id_type=MESH,
            ).wait_recv()

    @pl.when(owned)
    def _():
        past_here().wait()

    stored = past_buf[...].reshape(own * bunches, width)
    convolved = dot3(w_past, split(stored))

    whole(now_buf, now_send, now_recv).wait_recv()
    gathered = now_buf[...].reshape(sections, half, LANES)
    lower = lane_iota(half)[None] < width
    spread = jnp.concatenate(
        [jnp.where(lower, gathered, 0.0), jnp.where(lower, 0.0, gathered)], axis=1
    ).reshape(bunches_all, LANES)
    both = dot3(w_now, split(spread))
    convolved = convolved + (both[:, :width] + both[:, width:])
    conv_buf[d] = jnp.concatenate([convolved[:half], convolved[half:]], axis=1)
    dom_copies(conv_buf, conv_send, conv_recv)

    for copy in loads[5:]:
        copy.wait()
    to_kick = dot3(split(wake_in[...]), split(basis_buf[...]))
    to_kick = jnp.concatenate([to_kick, to_kick], axis=0)
    to_kick = split(to_kick)
    angle = phase_in[...]
    cosine, sine = jnp.cos(angle), jnp.sin(angle)
    for plane in range(2):
        row = 2 * bunches + 2 * plane
        out[row : row + 1, :] = jnp.broadcast_to(cosine[:, plane : plane + 1], (1, 2 * NBIN))
        out[row + 1 : row + 2, :] = jnp.broadcast_to(sine[:, plane : plane + 1], (1, 2 * NBIN))
    dom_wait = whole(dom_buf, dom_send, dom_recv)
    dom_wait.wait_recv()
    summed = dom_buf[0]
    for i in range(1, doms):
        summed = summed + dom_buf[i]
    summed = summed.reshape(half, LANES)
    out[bunches : bunches + half, 0:width] = summed[:, :width]
    out[bunches + half : 2 * bunches, 0:width] = summed[:, width:]

    @pl.when(owned)
    def _():
        for o in range(1, sections):
            past_copy(o).wait_send()

    whole(now_buf, now_send, now_recv).wait_send()
    dom_wait.wait_send()

    conv_wait = whole(conv_buf, conv_send, conv_recv)
    conv_wait.wait_recv()
    total = conv_buf[0]
    for i in range(1, doms):
        total = total + conv_buf[i]
    lower = lane_iota(half) < width
    total = jnp.concatenate([jnp.where(lower, total, 0.0), jnp.where(lower, 0.0, total)], axis=0)
    out[0:bunches, :] = dot3(split(total), to_kick)
    conv_wait.wait_send()


def track_kernel(particles, bins, table, tracked, moments_out, result, moments, sems):
    bunches, slots = bins.shape
    block = 16
    moments[...] = table[bunches : 2 * bunches, 0 : moments.shape[1]]
    through = pltpu.make_async_copy(moments, moments_out, sems.at[bunches // block])
    through.start()
    copies = []
    for i in range(bunches // block):
        rows = slice(i * block, (i + 1) * block)
        for plane in range(2):
            row = 2 * bunches + 2 * plane
            cosine = jnp.broadcast_to(table[row : row + 1, 0:LANES], (block, LANES))
            sine = jnp.broadcast_to(table[row + 1 : row + 2, 0:LANES], (block, LANES))
            kicks = table[rows, plane * NBIN : (plane + 1) * NBIN]
            for first in range(0, slots, LANES):
                here = slice(first, first + LANES)
                place = particles[2 * plane, rows, here]
                momentum = particles[2 * plane + 1, rows, here]
                kick = jnp.take_along_axis(
                    kicks, bins[rows, here], axis=1, mode="promise_in_bounds"
                )
                result[2 * plane, rows, here] = cosine * place + sine * momentum
                result[2 * plane + 1, rows, here] = cosine * momentum - sine * place + kick
        copy = pltpu.make_async_copy(result.at[:, rows, :], tracked.at[:, rows, :], sems.at[i])
        copy.start()
        copies.append(copy)
    for copy in copies:
        copy.wait()
    through.wait()


def local(sections, doms, particles, slice_bin, bunch_counts, past_moments, wake_lags, wake_matrix, adjust_phase):
    _, bunches, slots = particles.shape
    width = wake_matrix.shape[0]
    orders = width // 2
    half = bunches // 2
    chunks = half // 8
    bunches_all = bunches * sections
    own = 2 * sections // doms
    lag_rows = bunches_all // 32
    pad = pl.cdiv(bunches_all // 128, 8) * 8
    vmem = pl.BlockSpec(memory_space=pltpu.VMEM)
    hbm = pl.BlockSpec(memory_space=pltpu.HBM)
    dma = pltpu.SemaphoreType.DMA
    table = pl.pallas_call(
        functools.partial(moments_kernel, sections, doms, orders),
        out_shape=jax.ShapeDtypeStruct((2 * bunches + 8, 2 * NBIN), F32),
        in_specs=[hbm] * 7,
        out_specs=vmem,
        scratch_shapes=[
            pltpu.VMEM((bunches, slots), F32),
            pltpu.VMEM((bunches, slots), F32),
            pltpu.VMEM((bunches, slots), jnp.int32),
            pltpu.VMEM((1, bunches), jnp.int32),
            pltpu.VMEM(wake_lags.shape, F32),
            pltpu.VMEM((width, width), F32),
            pltpu.VMEM((1, 2), F32),
            pltpu.VMEM((pad + lag_rows, LANES), F32),
            pltpu.VMEM((width, 2 * NBIN), F32),
            pltpu.VMEM((bunches, LANES), F32),
            pltpu.VMEM((sections, chunks, 8, LANES), F32),
            pltpu.VMEM((own, bunches, width), F32),
            pltpu.VMEM((doms, chunks, 8, LANES), F32),
            pltpu.VMEM((doms, half, LANES), F32),
            dma((8,)),
            dma((sections - 1,)),
            dma((own,)),
            dma((6,)),
        ],
        compiler_params=pltpu.CompilerParams(
            collective_id=0, has_side_effects=True, vmem_limit_bytes=56 * 1024 * 1024
        ),
        name="moments",
    )(
        particles,
        slice_bin,
        bunch_counts.reshape(1, -1),
        past_moments,
        wake_lags,
        wake_matrix,
        adjust_phase.reshape(1, -1),
    )
    return pl.pallas_call(
        track_kernel,
        out_shape=(
            jax.ShapeDtypeStruct(particles.shape, F32),
            jax.ShapeDtypeStruct((bunches, width), F32),
        ),
        in_specs=[vmem, vmem, vmem],
        out_specs=(hbm, hbm),
        scratch_shapes=[pltpu.VMEM(particles.shape, F32), pltpu.VMEM((bunches, width), F32), dma((bunches // 16 + 1,))],
        compiler_params=pltpu.CompilerParams(vmem_limit_bytes=16 * 1024 * 1024),
        name="track",
    )(particles, slice_bin, table)


def solution(mesh):
    in_specs = (
        P(None, "train", "dom"),
        P("train", "dom"),
        P("train"),
        P(None, "train", None),
        P(),
        P(),
        P(),
    )
    out_specs = (P(None, "train", "dom"), P("train", None))
    body = functools.partial(local, mesh.shape["train"], mesh.shape["dom"])
    return jax.shard_map(body, mesh=mesh, in_specs=in_specs, out_specs=out_specs, check_vma=False)
```

```python
import functools

import jax
import jax.numpy as jnp
import numpy as np
from jax import lax
from jax.experimental import pallas as pl
from jax.experimental.pallas import tpu as pltpu
from jax.sharding import PartitionSpec as P

NBIN = 128
LANES = 128
MESH = pl.DeviceIdType.MESH
F32 = jnp.float32
BF16 = jnp.bfloat16


def split(a):
    high = a.astype(BF16)
    return high, (a - high.astype(F32)).astype(BF16)


def dot(a, b):
    return jnp.dot(a, b, preferred_element_type=F32)


def dot3(a_parts, b_parts):
    (ah, al), (bh, bl) = a_parts, b_parts
    return dot(ah, bh) + (dot(ah, bl) + dot(al, bh))


def lane_iota(rows):
    return lax.broadcasted_iota(jnp.int32, (rows, LANES), 1)


def merge(a, b, distance):
    low = (lane_iota(a.shape[0]) & distance) == 0
    return jnp.where(low, a, b) + pltpu.roll(jnp.where(low, b, a), distance, 1)


def product_basis(orders):
    nodes = np.cos((np.arange(orders) + 0.5) * np.pi / orders)
    angle = np.arccos(nodes)
    outer = orders // 8
    products = np.stack(
        [np.cos(8 * a * angle) * np.cos(j * angle) for j in range(8) for a in range(outer)], 1
    )
    legendre = np.polynomial.legendre.legvander(nodes, orders - 1)
    return np.linalg.solve(products, legendre) * (2 * np.arange(orders) + 1)


def plane_maps(orders):
    outer = orders // 8
    one = product_basis(orders)
    both = np.zeros((2 * orders, 2 * orders))
    for c in range(2):
        for j in range(8):
            for a in range(outer):
                both[(j * 2 + c) * outer + a, c * orders : (c + 1) * orders] = one[j * outer + a]
    twice = np.kron(np.eye(2), both)
    return [m.astype(np.float32) for m in (both, np.linalg.inv(both), twice)]


def tile_sum(a):
    parts = [a[:, i : i + LANES] for i in range(0, a.shape[1], LANES)]
    while len(parts) > 1:
        parts = [p + q for p, q in zip(parts[::2], parts[1::2])] + parts[len(parts) & ~1 :]
    return parts[0]


def moments_kernel(
    sections, doms, orders,
    particles, bins, counts, past, lags, wake, phase, to_moments, to_raw, to_both,
    out,
    x_buf, y_buf, bin_buf, count_in, lag_in, wake_in, phase_in, to_moments_in, to_raw_in, to_both_in, e_buf, basis_buf, count_buf,
    now_buf, past_buf, dom_buf, conv_buf,
    load_sem, past_send, past_recv, pair_sem,
):
    bunches = counts.shape[1]
    half = bunches // 2
    chunks = half // 8
    width = 2 * orders
    bunches_all = bunches * sections
    own = 2 * sections // doms
    t = lax.axis_index("train")
    d = lax.axis_index("dom")
    now_send, now_recv, dom_send, dom_recv, conv_send, conv_recv = [pair_sem.at[i] for i in range(6)]

    barrier = pltpu.get_barrier_semaphore()
    for o in range(1, sections):
        pl.semaphore_signal(
            barrier, inc=1, device_id=(lax.rem(t + o, sections), d), device_id_type=MESH
        )
    for o in range(1, doms):
        pl.semaphore_signal(
            barrier, inc=1, device_id=(t, lax.rem(d + o, doms)), device_id_type=MESH
        )
    pairs = [
        (counts, count_in),
        (bins, bin_buf),
        (particles.at[0], x_buf),
        (particles.at[2], y_buf),
        (lags, lag_in),
        (wake, wake_in),
        (phase, phase_in),
        (to_moments, to_moments_in),
        (to_raw, to_raw_in),
        (to_both, to_both_in),
    ]
    loads = [
        pltpu.make_async_copy(src, dst, load_sem.at[i]) for i, (src, dst) in enumerate(pairs)
    ]
    for copy in loads:
        copy.start()

    late = t // own == d
    owned = jnp.logical_or(late, (sections + t) // own == d)
    turn = jnp.where(late, 1, 0)
    slot = lax.rem(t, own)

    def past_copy(o):
        return pltpu.make_async_remote_copy(
            src_ref=past.at[turn], dst_ref=past_buf.at[slot],
            send_sem=past_send.at[o - 1], recv_sem=past_recv.at[slot],
            device_id=(lax.rem(t + o, sections), d), device_id_type=MESH,
        )

    def past_here():
        return pltpu.make_async_copy(past.at[turn], past_buf.at[slot], load_sem.at[len(pairs)])

    @pl.when(owned)
    def _():
        past_here().start()

    basis_buf[...] = jnp.zeros_like(basis_buf)
    centers = (lane_iota(1).astype(F32) + 0.5) * (2.0 / NBIN) - 1.0
    previous, current = jnp.ones_like(centers), centers
    for k in range(orders):
        basis_buf[k : k + 1, 0:LANES] = previous
        basis_buf[orders + k : orders + k + 1, LANES : 2 * LANES] = previous
        following = np.float32((2 * k + 3) / (k + 2)) * centers * current
        following = following - np.float32((k + 1) / (k + 2)) * previous
        previous, current = current, following

    loads[0].wait()
    eye = lax.broadcasted_iota(jnp.int32, (bunches, bunches), 0) == lax.broadcasted_iota(
        jnp.int32, (bunches, bunches), 1
    )
    count_f = count_in[...].astype(F32)
    column = jnp.sum(jnp.where(eye, count_f, 0.0), axis=1, keepdims=True)
    count_buf[...] = jnp.broadcast_to(column, (bunches, LANES))

    pl.semaphore_wait(barrier, sections - 1 + doms - 1)

    @pl.when(owned)
    def _():
        for o in range(1, sections):
            past_copy(o).start()

    for copy in loads[1:4]:
        copy.wait()
    slots = x_buf.shape[1]
    slot_index = d * slots + lax.broadcasted_iota(jnp.int32, (8, slots), 1)
    low_half = lane_iota(8) < width

    outer = orders // 8

    def group_sums(first):
        here = pl.ds(first, 8)
        count = count_buf[here, 0:1].astype(jnp.int32)
        piece = min(slots, 4 * LANES)
        sums = [[None] * (2 * outer) for _ in range(8)]
        for begin in range(0, slots, piece):
            part = slice(begin, begin + piece)
            z = (bin_buf[here, part].astype(F32) + 0.5) * (2.0 / NBIN) - 1.0
            twice = z + z
            alive = slot_index[:, part] < count
            vx = jnp.where(alive, x_buf[here, part], 0.0)
            vy = jnp.where(alive, y_buf[here, part], 0.0)
            t2 = twice * z - 1.0
            t4 = 2.0 * t2 * t2 - 1.0
            t8 = 2.0 * t4 * t4 - 1.0
            steps = [None, t8]
            for a in range(2, outer):
                steps.append(2.0 * t8 * steps[a - 1] - (1.0 if a == 2 else steps[a - 2]))
            streams = [v if a == 0 else v * steps[a] for v in (vx, vy) for a in range(outer)]
            before, at = None, None
            for j in range(8):
                if j == 1:
                    before, at = 1.0, z
                elif j > 1:
                    before, at = at, twice * at - before
                for i, stream in enumerate(streams):
                    term = tile_sum(stream if j == 0 else stream * at)
                    sums[j][i] = term if sums[j][i] is None else sums[j][i] + term
        values, distance = [value for row in sums for value in row], 1
        while len(values) > 1:
            values = [merge(p, q, distance) for p, q in zip(values[::2], values[1::2])]
            distance *= 2
        return values[0]

    def chunk(j, carry):
        first = pl.multiple_of(j * 8, 8)
        second = pl.multiple_of(j * 8 + half, 8)
        total = merge(group_sums(first), group_sums(second), width)
        divisor = jnp.where(
            low_half, count_buf[pl.ds(first, 8), :], count_buf[pl.ds(second, 8), :]
        )
        moments = total / divisor
        now_buf[t, j] = moments
        dom_buf[d, j] = moments
        for o in range(1, sections):
            pltpu.make_async_remote_copy(
                src_ref=now_buf.at[t, j], dst_ref=now_buf.at[t, j],
                send_sem=now_send, recv_sem=now_recv,
                device_id=(lax.rem(t + o, sections), d), device_id_type=MESH,
            ).start()
        return carry

    lax.fori_loop(0, chunks, chunk, 0)

    def dom_copies(ref, send_sem, recv_sem):
        for o in range(1, doms):
            pltpu.make_async_remote_copy(
                src_ref=ref.at[d], dst_ref=ref.at[d], send_sem=send_sem, recv_sem=recv_sem,
                device_id=(t, lax.rem(d + o, doms)), device_id_type=MESH,
            ).start()

    def whole(ref, send_sem, recv_sem):
        part = ref.at[pl.ds(0, ref.shape[0] - 1)]
        return pltpu.make_async_remote_copy(
            src_ref=part, dst_ref=part, send_sem=send_sem, recv_sem=recv_sem,
            device_id=(t, d), device_id_type=MESH,
        )

    dom_copies(dom_buf, dom_send, dom_recv)

    loads[4].wait()
    rows = bunches_all // 32
    pad = e_buf.shape[0] - rows
    count_lags = lag_in.shape[-1]
    e_buf[...] = jnp.zeros_like(e_buf)
    for row in range(pl.cdiv(count_lags, LANES)):
        size = min(LANES, count_lags - row * LANES)
        e_buf[pad + row : pad + row + 1, 0:size] = lag_in[pl.ds(row * LANES, size)].reshape(1, size)
    plain = e_buf[...]
    lane = lane_iota(plain.shape[0])
    turned = jnp.take_along_axis(plain, LANES - 1 - lane, axis=1, mode="promise_in_bounds")
    moved = pltpu.roll(turned, LANES // 2, 1)
    mixed = jnp.where(lane < LANES // 2, moved, pltpu.roll(moved, 1, 0))
    odd = lax.rem(t, 2)
    e_buf[...] = jnp.where(odd == 1, mixed, turned)
    first_row = pad + rows - 1 - bunches_all // 64 + (t + 1) // 2
    target = lax.broadcasted_iota(jnp.int32, (bunches, LANES), 0)
    source = lane_iota(bunches)

    def toeplitz(tile_first, tiles):
        def rolled(m):
            row = e_buf[pl.ds(first_row - m, 1), :]
            return pltpu.roll(
                jnp.broadcast_to(row, (bunches, LANES)), 0, 1, stride=1, stride_axis=0
            )

        turned_rows = [rolled(tile_first + m) for m in range(-1, tiles)]
        return jnp.concatenate(
            [
                jnp.where(source >= target, turned_rows[m + 1], turned_rows[m])
                for m in range(tiles)
            ],
            axis=1,
        )

    w_now = split(toeplitz(2 * bunches_all // LANES, bunches_all // LANES))
    past_tiles = own * bunches // LANES
    w_past = split(toeplitz(d * past_tiles, past_tiles))

    for s in range(own):
        @pl.when(lax.rem(d * own + s, sections) != t)
        def _():
            pltpu.make_async_remote_copy(
                src_ref=past.at[0], dst_ref=past_buf.at[s],
                send_sem=past_send.at[0], recv_sem=past_recv.at[s],
                device_id=(t, d), device_id_type=MESH,
            ).wait_recv()

    @pl.when(owned)
    def _():
        past_here().wait()

    stored = past_buf[...].reshape(own * bunches, width)
    for copy in loads[5:]:
        copy.wait()
    convolved = dot3(split(dot3(w_past, split(stored))), split(to_raw_in[...]))

    whole(now_buf, now_send, now_recv).wait_recv()
    gathered = now_buf[...].reshape(sections, half, LANES)
    lower = lane_iota(half)[None] < width
    spread = jnp.concatenate(
        [jnp.where(lower, gathered, 0.0), jnp.where(lower, 0.0, gathered)], axis=1
    ).reshape(bunches_all, LANES)
    both = dot3(w_now, split(spread))
    convolved = convolved + (both[:, :width] + both[:, width:])
    conv_buf[d] = jnp.concatenate([convolved[:half], convolved[half:]], axis=1)
    dom_copies(conv_buf, conv_send, conv_recv)

    to_kick = dot3(split(wake_in[...]), split(basis_buf[...]))
    to_kick = dot3(split(to_moments_in[...]), split(to_kick))
    to_kick = jnp.concatenate([to_kick, to_kick], axis=0)
    to_kick = split(to_kick)
    angle = phase_in[...]
    cosine, sine = jnp.cos(angle), jnp.sin(angle)
    for plane in range(2):
        row = 2 * bunches + 2 * plane
        out[row : row + 1, :] = jnp.broadcast_to(cosine[:, plane : plane + 1], (1, 2 * NBIN))
        out[row + 1 : row + 2, :] = jnp.broadcast_to(sine[:, plane : plane + 1], (1, 2 * NBIN))
    dom_wait = whole(dom_buf, dom_send, dom_recv)
    dom_wait.wait_recv()
    summed = dom_buf[0]
    for i in range(1, doms):
        summed = summed + dom_buf[i]
    summed = dot3(split(summed.reshape(half, LANES)), split(to_both_in[...]))
    out[bunches : bunches + half, 0:width] = summed[:, :width]
    out[bunches + half : 2 * bunches, 0:width] = summed[:, width:]

    @pl.when(owned)
    def _():
        for o in range(1, sections):
            past_copy(o).wait_send()

    whole(now_buf, now_send, now_recv).wait_send()
    dom_wait.wait_send()

    conv_wait = whole(conv_buf, conv_send, conv_recv)
    conv_wait.wait_recv()
    total = conv_buf[0]
    for i in range(1, doms):
        total = total + conv_buf[i]
    lower = lane_iota(half) < width
    total = jnp.concatenate([jnp.where(lower, total, 0.0), jnp.where(lower, 0.0, total)], axis=0)
    out[0:bunches, :] = dot3(split(total), to_kick)
    conv_wait.wait_send()


def track_kernel(particles, bins, table, tracked, moments_out, result, moments, sems):
    bunches, slots = bins.shape
    block = 16
    moments[...] = table[bunches : 2 * bunches, 0 : moments.shape[1]]
    through = pltpu.make_async_copy(moments, moments_out, sems.at[bunches // block])
    through.start()
    copies = []
    for i in range(bunches // block):
        rows = slice(i * block, (i + 1) * block)
        for plane in range(2):
            row = 2 * bunches + 2 * plane
            cosine = jnp.broadcast_to(table[row : row + 1, 0:LANES], (block, LANES))
            sine = jnp.broadcast_to(table[row + 1 : row + 2, 0:LANES], (block, LANES))
            kicks = table[rows, plane * NBIN : (plane + 1) * NBIN]
            for first in range(0, slots, LANES):
                here = slice(first, first + LANES)
                place = particles[2 * plane, rows, here]
                momentum = particles[2 * plane + 1, rows, here]
                kick = jnp.take_along_axis(
                    kicks, bins[rows, here], axis=1, mode="promise_in_bounds"
                )
                result[2 * plane, rows, here] = cosine * place + sine * momentum
                result[2 * plane + 1, rows, here] = cosine * momentum - sine * place + kick
        copy = pltpu.make_async_copy(result.at[:, rows, :], tracked.at[:, rows, :], sems.at[i])
        copy.start()
        copies.append(copy)
    for copy in copies:
        copy.wait()
    through.wait()


def local(sections, doms, particles, slice_bin, bunch_counts, past_moments, wake_lags, wake_matrix, adjust_phase):
    _, bunches, slots = particles.shape
    width = wake_matrix.shape[0]
    orders = width // 2
    half = bunches // 2
    chunks = half // 8
    bunches_all = bunches * sections
    own = 2 * sections // doms
    lag_rows = bunches_all // 32
    pad = pl.cdiv(bunches_all // 128, 8) * 8
    vmem = pl.BlockSpec(memory_space=pltpu.VMEM)
    hbm = pl.BlockSpec(memory_space=pltpu.HBM)
    dma = pltpu.SemaphoreType.DMA
    table = pl.pallas_call(
        functools.partial(moments_kernel, sections, doms, orders),
        out_shape=jax.ShapeDtypeStruct((2 * bunches + 8, 2 * NBIN), F32),
        in_specs=[hbm] * 10,
        out_specs=vmem,
        scratch_shapes=[
            pltpu.VMEM((bunches, slots), F32),
            pltpu.VMEM((bunches, slots), F32),
            pltpu.VMEM((bunches, slots), jnp.int32),
            pltpu.VMEM((1, bunches), jnp.int32),
            pltpu.VMEM(wake_lags.shape, F32),
            pltpu.VMEM((width, width), F32),
            pltpu.VMEM((1, 2), F32),
            pltpu.VMEM((width, width), F32),
            pltpu.VMEM((width, width), F32),
            pltpu.VMEM((2 * width, 2 * width), F32),
            pltpu.VMEM((pad + lag_rows, LANES), F32),
            pltpu.VMEM((width, 2 * NBIN), F32),
            pltpu.VMEM((bunches, LANES), F32),
            pltpu.VMEM((sections, chunks, 8, LANES), F32),
            pltpu.VMEM((own, bunches, width), F32),
            pltpu.VMEM((doms, chunks, 8, LANES), F32),
            pltpu.VMEM((doms, half, LANES), F32),
            dma((11,)),
            dma((sections - 1,)),
            dma((own,)),
            dma((6,)),
        ],
        compiler_params=pltpu.CompilerParams(
            collective_id=0, has_side_effects=True, vmem_limit_bytes=56 * 1024 * 1024
        ),
        name="moments",
    )(
        particles,
        slice_bin,
        bunch_counts.reshape(1, -1),
        past_moments,
        wake_lags,
        wake_matrix,
        adjust_phase.reshape(1, -1),
        *[jnp.asarray(m) for m in plane_maps(orders)],
    )
    return pl.pallas_call(
        track_kernel,
        out_shape=(
            jax.ShapeDtypeStruct(particles.shape, F32),
            jax.ShapeDtypeStruct((bunches, width), F32),
        ),
        in_specs=[vmem, vmem, vmem],
        out_specs=(hbm, hbm),
        scratch_shapes=[pltpu.VMEM(particles.shape, F32), pltpu.VMEM((bunches, width), F32), dma((bunches // 16 + 1,))],
        compiler_params=pltpu.CompilerParams(vmem_limit_bytes=16 * 1024 * 1024),
        name="track",
    )(particles, slice_bin, table)


def solution(mesh):
    in_specs = (
        P(None, "train", "dom"),
        P("train", "dom"),
        P("train"),
        P(None, "train", None),
        P(),
        P(),
        P(),
    )
    out_specs = (P(None, "train", "dom"), P("train", None))
    body = functools.partial(local, mesh.shape["train"], mesh.shape["dom"])
    return jax.shard_map(body, mesh=mesh, in_specs=in_specs, out_specs=out_specs, check_vma=False)
```

```python
import functools

import jax
import jax.numpy as jnp
import numpy as np
from jax import lax
from jax.experimental import pallas as pl
from jax.experimental.pallas import tpu as pltpu
from jax.sharding import PartitionSpec as P

NBIN = 128
LANES = 128
MESH = pl.DeviceIdType.MESH
F32 = jnp.float32
BF16 = jnp.bfloat16


def split(a):
    high = a.astype(BF16)
    return high, (a - high.astype(F32)).astype(BF16)


def dot(a, b):
    return jnp.dot(a, b, preferred_element_type=F32)


def dot3(a_parts, b_parts):
    (ah, al), (bh, bl) = a_parts, b_parts
    return dot(ah, bh) + (dot(ah, bl) + dot(al, bh))


def lane_iota(rows):
    return lax.broadcasted_iota(jnp.int32, (rows, LANES), 1)


def dot_t(a, b):
    return lax.dot_general(a, b, (((1,), (1,)), ((), ())), preferred_element_type=F32)


def dot3_t(a_parts, b_parts):
    (ah, al), (bh, bl) = a_parts, b_parts
    return dot_t(ah, bh) + (dot_t(ah, bl) + dot_t(al, bh))


def merge(a, b, distance, axis):
    low = (lax.broadcasted_iota(jnp.int32, a.shape, axis) & distance) == 0
    return jnp.where(low, a, b) + pltpu.roll(jnp.where(low, b, a), distance, axis)


def product_basis(orders):
    nodes = np.cos((np.arange(orders) + 0.5) * np.pi / orders)
    angle = np.arccos(nodes)
    outer = orders // 8
    products = np.stack(
        [np.cos(8 * a * angle) * np.cos(j * angle) for j in range(8) for a in range(outer)], 1
    )
    legendre = np.polynomial.legendre.legvander(nodes, orders - 1)
    return np.linalg.solve(products, legendre) * (2 * np.arange(orders) + 1)


def plane_maps(orders):
    outer = orders // 8
    one = product_basis(orders)
    both = np.zeros((2 * orders, 2 * orders))
    for c in range(2):
        for j in range(8):
            for a in range(outer):
                row = (j % 2) * orders + ((j // 2) * 2 + c) * outer + a
                both[row, c * orders : (c + 1) * orders] = one[j * outer + a]
    return both.astype(np.float32), np.linalg.inv(both).T.astype(np.float32)


def moments_kernel(
    sections, doms, orders,
    particles, bins, counts, past, lags, wake, phase, to_moments, to_raw,
    out,
    x_buf, y_buf, bin_buf, count_in, lag_in, wake_in, phase_in, to_moments_in, to_raw_in, e_buf, basis_buf,
    stream_buf, twice_buf, poly_buf,
    now_buf, past_buf, dom_buf, conv_buf,
    load_sem, past_send, past_recv, pair_sem,
):
    bunches = counts.shape[1]
    half = orders
    chunks = 4
    width = 2 * orders
    bunches_all = bunches * sections
    own = 2 * sections // doms
    t = lax.axis_index("train")
    d = lax.axis_index("dom")
    now_send, now_recv, dom_send, dom_recv, conv_send, conv_recv = [pair_sem.at[i] for i in range(6)]

    barrier = pltpu.get_barrier_semaphore()
    for o in range(1, sections):
        pl.semaphore_signal(
            barrier, inc=1, device_id=(lax.rem(t + o, sections), d), device_id_type=MESH
        )
    for o in range(1, doms):
        pl.semaphore_signal(
            barrier, inc=1, device_id=(t, lax.rem(d + o, doms)), device_id_type=MESH
        )
    pairs = [
        (counts, count_in),
        (bins, bin_buf),
        (particles.at[0], x_buf),
        (particles.at[2], y_buf),
        (lags, lag_in),
        (wake, wake_in),
        (phase, phase_in),
        (to_moments, to_moments_in),
        (to_raw, to_raw_in),
    ]
    loads = [
        pltpu.make_async_copy(src, dst, load_sem.at[i]) for i, (src, dst) in enumerate(pairs)
    ]
    for copy in loads:
        copy.start()

    late = t // own == d
    owned = jnp.logical_or(late, (sections + t) // own == d)
    turn = jnp.where(late, 1, 0)
    slot = lax.rem(t, own)

    def past_copy(o):
        return pltpu.make_async_remote_copy(
            src_ref=past.at[turn], dst_ref=past_buf.at[slot],
            send_sem=past_send.at[o - 1], recv_sem=past_recv.at[slot],
            device_id=(lax.rem(t + o, sections), d), device_id_type=MESH,
        )

    def past_here():
        return pltpu.make_async_copy(past.at[turn], past_buf.at[slot], load_sem.at[len(pairs)])

    @pl.when(owned)
    def _():
        past_here().start()

    basis_buf[...] = jnp.zeros_like(basis_buf)
    centers = (lane_iota(1).astype(F32) + 0.5) * (2.0 / NBIN) - 1.0
    previous, current = jnp.ones_like(centers), centers
    for k in range(orders):
        basis_buf[k : k + 1, 0:LANES] = previous
        basis_buf[orders + k : orders + k + 1, LANES : 2 * LANES] = previous
        following = np.float32((2 * k + 3) / (k + 2)) * centers * current
        following = following - np.float32((k + 1) / (k + 2)) * previous
        previous, current = current, following

    pl.semaphore_wait(barrier, sections - 1 + doms - 1)

    @pl.when(owned)
    def _():
        for o in range(1, sections):
            past_copy(o).start()

    for copy in loads[0:4]:
        copy.wait()
    slots = x_buf.shape[1]
    deep = slots // 2
    outer = orders // 8
    count = jnp.concatenate([count_in[...], count_in[...]], axis=1)
    slot_index = (
        d * slots
        + jnp.where(lane_iota(LANES) < bunches, 0, deep)
        + lax.broadcasted_iota(jnp.int32, (LANES, LANES), 0)
    )

    def upright(ref, first):
        return jnp.concatenate(
            [ref[:, first : first + LANES], ref[:, deep + first : deep + first + LANES]], axis=0
        ).T

    for first in range(0, deep, LANES):
        here = slice(first, first + LANES)
        z = (upright(bin_buf, first).astype(F32) + 0.5) * (2.0 / NBIN) - 1.0
        twice = z + z
        t2 = twice * z - 1.0
        t4 = 2.0 * t2 * t2 - 1.0
        t8 = 2.0 * t4 * t4 - 1.0
        twice_buf[here, :] = twice
        poly_buf[0, here, :] = jnp.ones_like(z)
        poly_buf[1, here, :] = z
        steps = [None, t8]
        for a in range(2, outer):
            steps.append(2.0 * t8 * steps[a - 1] - (1.0 if a == 2 else steps[a - 2]))
        alive = slot_index + first < count
        for c, ref in enumerate((x_buf, y_buf)):
            v = jnp.where(alive, upright(ref, first), 0.0)
            for a in range(outer):
                stream_buf[c * outer + a, here, :] = v if a == 0 else v * steps[a]

    unroll = 4
    count_f = count.astype(F32)
    for j in range(chunks):

        def rows_step(i, sums):
            sums = list(sums)
            for u in range(unroll):
                here = pl.ds(pl.multiple_of((i * unroll + u) * 8, 8), 8)
                even, odd = poly_buf[0, here, :], poly_buf[1, here, :]
                if j > 0:
                    twice = twice_buf[here, :]
                    even = twice * odd - even
                    odd = twice * even - odd
                    if j < chunks - 1:
                        poly_buf[0, here, :] = even
                        poly_buf[1, here, :] = odd
                for n in range(2 * outer):
                    stream = stream_buf[n, here, :]
                    sums[n] = sums[n] + (stream if j == 0 else stream * even)
                    sums[2 * outer + n] = sums[2 * outer + n] + stream * odd
            return tuple(sums)

        zero = jnp.zeros((8, LANES), F32)
        values = lax.fori_loop(0, deep // (8 * unroll), rows_step, (zero,) * (4 * outer))
        for distance in (1, 2, 4):
            values = [merge(p, q, distance, 0) for p, q in zip(values[::2], values[1::2])]
        moments = merge(values[0], values[1], width, 1) / count_f
        now_buf[t, j] = moments
        dom_buf[d, j] = moments
        for o in range(1, sections):
            pltpu.make_async_remote_copy(
                src_ref=now_buf.at[t, j], dst_ref=now_buf.at[t, j],
                send_sem=now_send, recv_sem=now_recv,
                device_id=(lax.rem(t + o, sections), d), device_id_type=MESH,
            ).start()

    def dom_copies(ref, send_sem, recv_sem):
        for o in range(1, doms):
            pltpu.make_async_remote_copy(
                src_ref=ref.at[d], dst_ref=ref.at[d], send_sem=send_sem, recv_sem=recv_sem,
                device_id=(t, lax.rem(d + o, doms)), device_id_type=MESH,
            ).start()

    def whole(ref, send_sem, recv_sem):
        part = ref.at[pl.ds(0, ref.shape[0] - 1)]
        return pltpu.make_async_remote_copy(
            src_ref=part, dst_ref=part, send_sem=send_sem, recv_sem=recv_sem,
            device_id=(t, d), device_id_type=MESH,
        )

    dom_copies(dom_buf, dom_send, dom_recv)

    loads[4].wait()
    rows = bunches_all // 32
    pad = e_buf.shape[0] - rows
    count_lags = lag_in.shape[-1]
    e_buf[...] = jnp.zeros_like(e_buf)
    for row in range(pl.cdiv(count_lags, LANES)):
        size = min(LANES, count_lags - row * LANES)
        e_buf[pad + row : pad + row + 1, 0:size] = lag_in[pl.ds(row * LANES, size)].reshape(1, size)
    plain = e_buf[...]
    lane = lane_iota(plain.shape[0])
    turned = jnp.take_along_axis(plain, LANES - 1 - lane, axis=1, mode="promise_in_bounds")
    moved = pltpu.roll(turned, LANES // 2, 1)
    mixed = jnp.where(lane < LANES // 2, moved, pltpu.roll(moved, 1, 0))
    odd = lax.rem(t, 2)
    e_buf[...] = jnp.where(odd == 1, mixed, turned)
    first_row = pad + rows - 1 - bunches_all // 64 + (t + 1) // 2
    target = lax.broadcasted_iota(jnp.int32, (bunches, LANES), 0)
    source = lane_iota(bunches)

    def toeplitz(tile_first, tiles):
        def rolled(m):
            row = e_buf[pl.ds(first_row - m, 1), :]
            return pltpu.roll(
                jnp.broadcast_to(row, (bunches, LANES)), 0, 1, stride=1, stride_axis=0
            )

        turned_rows = [rolled(tile_first + m) for m in range(-1, tiles)]
        return [
            jnp.where(source >= target, turned_rows[m + 1], turned_rows[m]) for m in range(tiles)
        ]

    low = source < bunches
    above, below = [], []
    for tile in toeplitz(2 * bunches_all // LANES, bunches_all // LANES):
        swapped = pltpu.roll(tile, LANES // 2, 1)
        above += [jnp.where(low, tile, 0.0), jnp.where(low, swapped, 0.0)]
        below += [jnp.where(low, 0.0, swapped), jnp.where(low, 0.0, tile)]
    w_now = split(
        jnp.concatenate([jnp.concatenate(above, axis=1), jnp.concatenate(below, axis=1)], axis=0)
    )
    past_tiles = own * bunches // LANES
    w_past = split(jnp.concatenate(toeplitz(d * past_tiles, past_tiles), axis=1))

    for s in range(own):
        @pl.when(lax.rem(d * own + s, sections) != t)
        def _():
            pltpu.make_async_remote_copy(
                src_ref=past.at[0], dst_ref=past_buf.at[s],
                send_sem=past_send.at[0], recv_sem=past_recv.at[s],
                device_id=(t, d), device_id_type=MESH,
            ).wait_recv()

    @pl.when(owned)
    def _():
        past_here().wait()

    stored = past_buf[...].reshape(own * bunches, width)
    for copy in loads[5:]:
        copy.wait()
    raw = dot3_t(split(to_raw_in[...]), split(dot3(w_past, split(stored))))
    convolved = jnp.concatenate([raw[:half], raw[half:]], axis=1)

    whole(now_buf, now_send, now_recv).wait_recv()
    gathered = jnp.concatenate(
        [now_buf[i].reshape(half, LANES) for i in range(sections)], axis=1
    )
    conv_buf[d] = convolved + dot3_t(split(gathered), w_now)
    dom_copies(conv_buf, conv_send, conv_recv)

    to_kick = dot3(split(wake_in[...]), split(basis_buf[...]))
    to_kick = dot3(split(to_moments_in[...]), split(to_kick))
    to_kick = split(to_kick[:half]), split(to_kick[half:])
    angle = phase_in[...]
    cosine, sine = jnp.cos(angle), jnp.sin(angle)
    for plane in range(2):
        row = 2 * bunches + 2 * plane
        out[row : row + 1, :] = jnp.broadcast_to(cosine[:, plane : plane + 1], (1, 2 * NBIN))
        out[row + 1 : row + 2, :] = jnp.broadcast_to(sine[:, plane : plane + 1], (1, 2 * NBIN))
    dom_wait = whole(dom_buf, dom_send, dom_recv)
    dom_wait.wait_recv()
    summed = dom_buf[0]
    for i in range(1, doms):
        summed = summed + dom_buf[i]
    def from_packed(packed, maps):
        turned = packed.T
        return dot3(split(turned[:bunches]), maps[0]) + dot3(split(turned[bunches:]), maps[1])

    to_moments_parts = split(to_moments_in[0:half, :]), split(to_moments_in[half:width, :])
    out[bunches : 2 * bunches, 0:width] = from_packed(
        summed.reshape(half, LANES), to_moments_parts
    )

    @pl.when(owned)
    def _():
        for o in range(1, sections):
            past_copy(o).wait_send()

    whole(now_buf, now_send, now_recv).wait_send()
    dom_wait.wait_send()

    conv_wait = whole(conv_buf, conv_send, conv_recv)
    conv_wait.wait_recv()
    total = conv_buf[0]
    for i in range(1, doms):
        total = total + conv_buf[i]
    out[0:bunches, :] = from_packed(total, to_kick)
    conv_wait.wait_send()


def track_kernel(particles, bins, table, tracked, moments_out, result, moments, sems):
    bunches, slots = bins.shape
    block = 16
    moments[...] = table[bunches : 2 * bunches, 0 : moments.shape[1]]
    through = pltpu.make_async_copy(moments, moments_out, sems.at[bunches // block])
    through.start()
    copies = []
    for i in range(bunches // block):
        rows = slice(i * block, (i + 1) * block)
        for plane in range(2):
            row = 2 * bunches + 2 * plane
            cosine = jnp.broadcast_to(table[row : row + 1, 0:LANES], (block, LANES))
            sine = jnp.broadcast_to(table[row + 1 : row + 2, 0:LANES], (block, LANES))
            kicks = table[rows, plane * NBIN : (plane + 1) * NBIN]
            for first in range(0, slots, LANES):
                here = slice(first, first + LANES)
                place = particles[2 * plane, rows, here]
                momentum = particles[2 * plane + 1, rows, here]
                kick = jnp.take_along_axis(
                    kicks, bins[rows, here], axis=1, mode="promise_in_bounds"
                )
                result[2 * plane, rows, here] = cosine * place + sine * momentum
                result[2 * plane + 1, rows, here] = cosine * momentum - sine * place + kick
        copy = pltpu.make_async_copy(result.at[:, rows, :], tracked.at[:, rows, :], sems.at[i])
        copy.start()
        copies.append(copy)
    for copy in copies:
        copy.wait()
    through.wait()


def local(sections, doms, particles, slice_bin, bunch_counts, past_moments, wake_lags, wake_matrix, adjust_phase):
    _, bunches, slots = particles.shape
    width = wake_matrix.shape[0]
    orders = width // 2
    half = orders
    chunks = 4
    bunches_all = bunches * sections
    own = 2 * sections // doms
    lag_rows = bunches_all // 32
    pad = pl.cdiv(bunches_all // 128, 8) * 8
    vmem = pl.BlockSpec(memory_space=pltpu.VMEM)
    hbm = pl.BlockSpec(memory_space=pltpu.HBM)
    dma = pltpu.SemaphoreType.DMA
    table = pl.pallas_call(
        functools.partial(moments_kernel, sections, doms, orders),
        out_shape=jax.ShapeDtypeStruct((2 * bunches + 8, 2 * NBIN), F32),
        in_specs=[hbm] * 9,
        out_specs=vmem,
        scratch_shapes=[
            pltpu.VMEM((bunches, slots), F32),
            pltpu.VMEM((bunches, slots), F32),
            pltpu.VMEM((bunches, slots), jnp.int32),
            pltpu.VMEM((1, bunches), jnp.int32),
            pltpu.VMEM(wake_lags.shape, F32),
            pltpu.VMEM((width, width), F32),
            pltpu.VMEM((1, 2), F32),
            pltpu.VMEM((width, width), F32),
            pltpu.VMEM((width, width), F32),
            pltpu.VMEM((pad + lag_rows, LANES), F32),
            pltpu.VMEM((width, 2 * NBIN), F32),
            pltpu.VMEM((width // 8, slots // 2, LANES), F32),
            pltpu.VMEM((slots // 2, LANES), F32),
            pltpu.VMEM((2, slots // 2, LANES), F32),
            pltpu.VMEM((sections, chunks, 8, LANES), F32),
            pltpu.VMEM((own, bunches, width), F32),
            pltpu.VMEM((doms, chunks, 8, LANES), F32),
            pltpu.VMEM((doms, half, LANES), F32),
            dma((10,)),
            dma((sections - 1,)),
            dma((own,)),
            dma((6,)),
        ],
        compiler_params=pltpu.CompilerParams(
            collective_id=0, has_side_effects=True, vmem_limit_bytes=56 * 1024 * 1024
        ),
        name="moments",
    )(
        particles,
        slice_bin,
        bunch_counts.reshape(1, -1),
        past_moments,
        wake_lags,
        wake_matrix,
        adjust_phase.reshape(1, -1),
        *[jnp.asarray(m) for m in plane_maps(orders)],
    )
    return pl.pallas_call(
        track_kernel,
        out_shape=(
            jax.ShapeDtypeStruct(particles.shape, F32),
            jax.ShapeDtypeStruct((bunches, width), F32),
        ),
        in_specs=[vmem, vmem, vmem],
        out_specs=(hbm, hbm),
        scratch_shapes=[pltpu.VMEM(particles.shape, F32), pltpu.VMEM((bunches, width), F32), dma((bunches // 16 + 1,))],
        compiler_params=pltpu.CompilerParams(vmem_limit_bytes=16 * 1024 * 1024),
        name="track",
    )(particles, slice_bin, table)


def solution(mesh):
    in_specs = (
        P(None, "train", "dom"),
        P("train", "dom"),
        P("train"),
        P(None, "train", None),
        P(),
        P(),
        P(),
    )
    out_specs = (P(None, "train", "dom"), P("train", None))
    body = functools.partial(local, mesh.shape["train"], mesh.shape["dom"])
    return jax.shard_map(body, mesh=mesh, in_specs=in_specs, out_specs=out_specs, check_vma=False)
```

```python
import functools

import jax
import jax.numpy as jnp
import numpy as np
from jax import lax
from jax.experimental import pallas as pl
from jax.experimental.pallas import tpu as pltpu
from jax.sharding import PartitionSpec as P

NBIN = 128
LANES = 128
MESH = pl.DeviceIdType.MESH
F32 = jnp.float32
BF16 = jnp.bfloat16


def split(a):
    high = a.astype(BF16)
    return high, (a - high.astype(F32)).astype(BF16)


def dot(a, b):
    return jnp.dot(a, b, preferred_element_type=F32)


def dot3(a_parts, b_parts):
    (ah, al), (bh, bl) = a_parts, b_parts
    return dot(ah, bh) + (dot(ah, bl) + dot(al, bh))


def lane_iota(rows):
    return lax.broadcasted_iota(jnp.int32, (rows, LANES), 1)


def dot_t(a, b):
    return lax.dot_general(a, b, (((1,), (1,)), ((), ())), preferred_element_type=F32)


def dot3_t(a_parts, b_parts):
    (ah, al), (bh, bl) = a_parts, b_parts
    return dot_t(ah, bh) + (dot_t(ah, bl) + dot_t(al, bh))


def merge(a, b, distance, axis):
    low = (lax.broadcasted_iota(jnp.int32, a.shape, axis) & distance) == 0
    return jnp.where(low, a, b) + pltpu.roll(jnp.where(low, b, a), distance, axis)


def product_basis(orders):
    nodes = np.cos((np.arange(orders) + 0.5) * np.pi / orders)
    angle = np.arccos(nodes)
    outer = orders // 8
    products = np.stack(
        [np.cos(8 * a * angle) * np.cos(j * angle) for j in range(8) for a in range(outer)], 1
    )
    legendre = np.polynomial.legendre.legvander(nodes, orders - 1)
    return np.linalg.solve(products, legendre) * (2 * np.arange(orders) + 1)


def plane_maps(orders):
    outer = orders // 8
    one = product_basis(orders)
    both = np.zeros((2 * orders, 2 * orders))
    for c in range(2):
        for j in range(8):
            for a in range(outer):
                row = (j % 2) * orders + ((j // 2) * 2 + c) * outer + a
                both[row, c * orders : (c + 1) * orders] = one[j * outer + a]
    return both.astype(np.float32), np.linalg.inv(both).T.astype(np.float32)


def moments_kernel(
    sections, doms, orders,
    particles, bins, counts, past, lags, wake, phase, to_moments, to_raw,
    out,
    x_buf, y_buf, bin_buf, count_in, lag_in, wake_in, phase_in, to_moments_in, to_raw_in, e_buf, basis_buf,
    stream_buf, twice_buf, poly_buf,
    now_buf, past_in, past_mine, past_buf, part_mine, part_buf, share_mine, share_buf, dom_buf, conv_buf,
    load_sem, past_send, past_recv, pair_sem,
):
    bunches = counts.shape[1]
    half = orders
    chunks = 4
    width = 2 * orders
    bunches_all = bunches * sections
    own = 2 * sections // doms
    t = lax.axis_index("train")
    d = lax.axis_index("dom")
    part_sems, now_sems, dom_sems, share_sems, conv_sems = [
        (pair_sem.at[2 * i], pair_sem.at[2 * i + 1]) for i in range(5)
    ]
    pieces = doms // chunks
    piece_rows = half // doms

    barrier = pltpu.get_barrier_semaphore()
    for o in range(1, sections):
        pl.semaphore_signal(
            barrier, inc=1, device_id=(lax.rem(t + o, sections), d), device_id_type=MESH
        )
    for o in range(1, doms):
        pl.semaphore_signal(
            barrier, inc=1, device_id=(t, lax.rem(d + o, doms)), device_id_type=MESH
        )
    pairs = [
        (counts, count_in),
        (bins, bin_buf),
        (particles.at[0], x_buf),
        (particles.at[2], y_buf),
        (lags, lag_in),
        (wake, wake_in),
        (phase, phase_in),
        (to_moments, to_moments_in),
        (to_raw, to_raw_in),
    ]
    loads = [
        pltpu.make_async_copy(src, dst, load_sem.at[i]) for i, (src, dst) in enumerate(pairs)
    ]
    for copy in loads:
        copy.start()

    late = t // own == d
    owned = jnp.logical_or(late, (sections + t) // own == d)
    turn = jnp.where(late, 1, 0)
    slot = lax.rem(t, own)

    def past_copy(o):
        return pltpu.make_async_remote_copy(
            src_ref=past_mine, dst_ref=past_buf.at[slot],
            send_sem=past_send.at[o - 1], recv_sem=past_recv.at[slot],
            device_id=(lax.rem(t + o, sections), d), device_id_type=MESH,
        )

    def past_here():
        return pltpu.make_async_copy(past.at[turn], past_in, load_sem.at[len(pairs)])

    @pl.when(owned)
    def _():
        past_here().start()

    basis_buf[...] = jnp.zeros_like(basis_buf)
    centers = (lane_iota(1).astype(F32) + 0.5) * (2.0 / NBIN) - 1.0
    previous, current = jnp.ones_like(centers), centers
    for k in range(orders):
        basis_buf[k : k + 1, 0:LANES] = previous
        basis_buf[orders + k : orders + k + 1, LANES : 2 * LANES] = previous
        following = np.float32((2 * k + 3) / (k + 2)) * centers * current
        following = following - np.float32((k + 1) / (k + 2)) * previous
        previous, current = current, following

    pl.semaphore_wait(barrier, sections - 1 + doms - 1)

    @pl.when(owned)
    def _():
        past_here().wait()
        block = past_in[...]
        block = jnp.concatenate([block[: bunches // 2], block[bunches // 2 :]], axis=1)
        past_mine[...] = block
        past_buf[slot] = block
        for o in range(1, sections):
            past_copy(o).start()

    for copy in loads[0:4]:
        copy.wait()
    slots = x_buf.shape[1]
    deep = slots // 2
    outer = orders // 8
    count = jnp.concatenate([count_in[...], count_in[...]], axis=1)
    slot_index = (
        d * slots
        + jnp.where(lane_iota(LANES) < bunches, 0, deep)
        + lax.broadcasted_iota(jnp.int32, (LANES, LANES), 0)
    )

    def upright(ref, first):
        return jnp.concatenate(
            [ref[:, first : first + LANES], ref[:, deep + first : deep + first + LANES]], axis=0
        ).T

    for first in range(0, deep, LANES):
        here = slice(first, first + LANES)
        z = (upright(bin_buf, first).astype(F32) + 0.5) * (2.0 / NBIN) - 1.0
        twice = z + z
        t2 = twice * z - 1.0
        t4 = 2.0 * t2 * t2 - 1.0
        t8 = 2.0 * t4 * t4 - 1.0
        twice_buf[here, :] = twice
        poly_buf[0, here, :] = jnp.ones_like(z)
        poly_buf[1, here, :] = z
        steps = [None, t8]
        for a in range(2, outer):
            steps.append(2.0 * t8 * steps[a - 1] - (1.0 if a == 2 else steps[a - 2]))
        alive = slot_index + first < count
        for c, ref in enumerate((x_buf, y_buf)):
            v = jnp.where(alive, upright(ref, first), 0.0)
            for a in range(outer):
                stream_buf[c * outer + a, here, :] = v if a == 0 else v * steps[a]

    def dom_copies(ref, sems):
        for o in range(1, doms):
            pltpu.make_async_remote_copy(
                src_ref=ref.at[d], dst_ref=ref.at[d], send_sem=sems[0], recv_sem=sems[1],
                device_id=(t, lax.rem(d + o, doms)), device_id_type=MESH,
            ).start()

    def to_piece(mine, buf, sems, e):
        @pl.when(d != e)
        def _():
            pltpu.make_async_remote_copy(
                src_ref=mine.at[e], dst_ref=buf.at[d], send_sem=sems[0], recv_sem=sems[1],
                device_id=(t, e), device_id_type=MESH,
            ).start()

    def whole(ref, sems):
        part = ref.at[pl.ds(0, ref.shape[0] - 1)]
        return pltpu.make_async_remote_copy(
            src_ref=part, dst_ref=part, send_sem=sems[0], recv_sem=sems[1],
            device_id=(t, d), device_id_type=MESH,
        )

    unroll = 4
    count_f = count.astype(F32)
    for j in range(chunks):

        def rows_step(i, sums):
            sums = list(sums)
            for u in range(unroll):
                here = pl.ds(pl.multiple_of((i * unroll + u) * 8, 8), 8)
                even, odd = poly_buf[0, here, :], poly_buf[1, here, :]
                if j > 0:
                    twice = twice_buf[here, :]
                    even = twice * odd - even
                    odd = twice * even - odd
                    if j < chunks - 1:
                        poly_buf[0, here, :] = even
                        poly_buf[1, here, :] = odd
                for n in range(2 * outer):
                    stream = stream_buf[n, here, :]
                    sums[n] = sums[n] + (stream if j == 0 else stream * even)
                    sums[2 * outer + n] = sums[2 * outer + n] + stream * odd
            return tuple(sums)

        zero = jnp.zeros((8, LANES), F32)
        values = lax.fori_loop(0, deep // (8 * unroll), rows_step, (zero,) * (4 * outer))
        for distance in (1, 2, 4):
            values = [merge(p, q, distance, 0) for p, q in zip(values[::2], values[1::2])]
        moments = merge(values[0], values[1], width, 1)
        for i in range(pieces):
            e = j * pieces + i
            part_mine[e] = moments[i * piece_rows : (i + 1) * piece_rows]
            to_piece(part_mine, part_buf, part_sems, e)

    for copy in loads[5:]:
        copy.wait()
    to_kick = dot3(split(wake_in[...]), split(basis_buf[...]))
    to_kick = dot3(split(to_moments_in[...]), split(to_kick))
    to_kick = split(to_kick[:half]), split(to_kick[half:])
    angle = phase_in[...]
    cosine, sine = jnp.cos(angle), jnp.sin(angle)
    for plane in range(2):
        row = 2 * bunches + 2 * plane
        out[row : row + 1, :] = jnp.broadcast_to(cosine[:, plane : plane + 1], (1, 2 * NBIN))
        out[row + 1 : row + 2, :] = jnp.broadcast_to(sine[:, plane : plane + 1], (1, 2 * NBIN))

    part_buf[d] = part_mine[d]
    part_wait = whole(part_buf, part_sems)
    part_wait.wait_recv()
    reduced = part_buf[0]
    for i in range(1, doms):
        reduced = reduced + part_buf[i]
    reduced = reduced / count_f
    now_buf[t] = reduced
    dom_buf[d] = reduced
    for o in range(1, sections):
        pltpu.make_async_remote_copy(
            src_ref=now_buf.at[t], dst_ref=now_buf.at[t],
            send_sem=now_sems[0], recv_sem=now_sems[1],
            device_id=(lax.rem(t + o, sections), d), device_id_type=MESH,
        ).start()
    dom_copies(dom_buf, dom_sems)

    loads[4].wait()
    rows = bunches_all // 32
    pad = e_buf.shape[0] - rows
    count_lags = lag_in.shape[-1]
    e_buf[...] = jnp.zeros_like(e_buf)
    for row in range(pl.cdiv(count_lags, LANES)):
        size = min(LANES, count_lags - row * LANES)
        e_buf[pad + row : pad + row + 1, 0:size] = lag_in[pl.ds(row * LANES, size)].reshape(1, size)
    plain = e_buf[...]
    lane = lane_iota(plain.shape[0])
    turned = jnp.take_along_axis(plain, LANES - 1 - lane, axis=1, mode="promise_in_bounds")
    moved = pltpu.roll(turned, LANES // 2, 1)
    mixed = jnp.where(lane < LANES // 2, moved, pltpu.roll(moved, 1, 0))
    odd = lax.rem(t, 2)
    e_buf[...] = jnp.where(odd == 1, mixed, turned)
    first_row = pad + rows - 1 - bunches_all // 64 + (t + 1) // 2
    target = lax.broadcasted_iota(jnp.int32, (bunches, LANES), 0)
    source = lane_iota(bunches)

    def toeplitz(tile_first, tiles):
        def rolled(m):
            row = e_buf[pl.ds(first_row - m, 1), :]
            return pltpu.roll(
                jnp.broadcast_to(row, (bunches, LANES)), 0, 1, stride=1, stride_axis=0
            )

        turned_rows = [rolled(tile_first + m) for m in range(-1, tiles)]
        return [
            jnp.where(source >= target, turned_rows[m + 1], turned_rows[m]) for m in range(tiles)
        ]

    low = source < bunches
    above, below = [], []
    for tile in toeplitz(2 * bunches_all // LANES, bunches_all // LANES):
        swapped = pltpu.roll(tile, LANES // 2, 1)
        above += [jnp.where(low, tile, 0.0), jnp.where(low, swapped, 0.0)]
        below += [jnp.where(low, 0.0, swapped), jnp.where(low, 0.0, tile)]
    w_now = split(
        jnp.concatenate([jnp.concatenate(above, axis=1), jnp.concatenate(below, axis=1)], axis=0)
    )
    past_tiles = own * bunches // LANES
    w_past = split(jnp.concatenate(toeplitz(d * past_tiles, past_tiles), axis=1))

    for s in range(own):
        @pl.when(lax.rem(d * own + s, sections) != t)
        def _():
            pltpu.make_async_remote_copy(
                src_ref=past_mine, dst_ref=past_buf.at[s],
                send_sem=past_send.at[0], recv_sem=past_recv.at[s],
                device_id=(t, d), device_id_type=MESH,
            ).wait_recv()

    stored = jnp.concatenate(
        [past_buf[i][:, side * width : (side + 1) * width] for i in range(own) for side in range(2)],
        axis=0,
    )
    raw = dot3_t(split(to_raw_in[...]), split(dot3(w_past, split(stored))))
    convolved = jnp.concatenate([raw[:half], raw[half:]], axis=1)

    for e in range(doms):
        share_mine[e] = convolved[e * piece_rows : (e + 1) * piece_rows]
        to_piece(share_mine, share_buf, share_sems, e)
    share_buf[d] = share_mine[d]

    now_wait = whole(now_buf, now_sems)
    now_wait.wait_recv()
    gathered = jnp.concatenate([now_buf[i] for i in range(sections)], axis=1)
    convolved = dot3_t(split(gathered), w_now)
    share_wait = whole(share_buf, share_sems)
    share_wait.wait_recv()
    for i in range(doms):
        convolved = convolved + share_buf[i]
    conv_buf[d] = convolved
    dom_copies(conv_buf, conv_sems)

    dom_wait = whole(dom_buf, dom_sems)
    dom_wait.wait_recv()
    def from_packed(packed, maps):
        turned = packed.T
        return dot3(split(turned[:bunches]), maps[0]) + dot3(split(turned[bunches:]), maps[1])

    to_moments_parts = split(to_moments_in[0:half, :]), split(to_moments_in[half:width, :])
    out[bunches : 2 * bunches, 0:width] = from_packed(
        dom_buf[...].reshape(half, LANES), to_moments_parts
    )

    @pl.when(owned)
    def _():
        for o in range(1, sections):
            past_copy(o).wait_send()

    for copy in (part_wait, now_wait, dom_wait, share_wait):
        copy.wait_send()

    conv_wait = whole(conv_buf, conv_sems)
    conv_wait.wait_recv()
    total = conv_buf[...].reshape(half, LANES)
    out[0:bunches, :] = from_packed(total, to_kick)
    conv_wait.wait_send()


def track_kernel(particles, bins, table, tracked, moments_out, result, moments, sems):
    bunches, slots = bins.shape
    block = 16
    moments[...] = table[bunches : 2 * bunches, 0 : moments.shape[1]]
    through = pltpu.make_async_copy(moments, moments_out, sems.at[bunches // block])
    through.start()
    copies = []
    for i in range(bunches // block):
        rows = slice(i * block, (i + 1) * block)
        for plane in range(2):
            row = 2 * bunches + 2 * plane
            cosine = jnp.broadcast_to(table[row : row + 1, 0:LANES], (block, LANES))
            sine = jnp.broadcast_to(table[row + 1 : row + 2, 0:LANES], (block, LANES))
            kicks = table[rows, plane * NBIN : (plane + 1) * NBIN]
            for first in range(0, slots, LANES):
                here = slice(first, first + LANES)
                place = particles[2 * plane, rows, here]
                momentum = particles[2 * plane + 1, rows, here]
                kick = jnp.take_along_axis(
                    kicks, bins[rows, here], axis=1, mode="promise_in_bounds"
                )
                result[2 * plane, rows, here] = cosine * place + sine * momentum
                result[2 * plane + 1, rows, here] = cosine * momentum - sine * place + kick
        copy = pltpu.make_async_copy(result.at[:, rows, :], tracked.at[:, rows, :], sems.at[i])
        copy.start()
        copies.append(copy)
    for copy in copies:
        copy.wait()
    through.wait()


def local(sections, doms, particles, slice_bin, bunch_counts, past_moments, wake_lags, wake_matrix, adjust_phase):
    _, bunches, slots = particles.shape
    width = wake_matrix.shape[0]
    orders = width // 2
    half = orders
    bunches_all = bunches * sections
    own = 2 * sections // doms
    lag_rows = bunches_all // 32
    pad = pl.cdiv(bunches_all // 128, 8) * 8
    vmem = pl.BlockSpec(memory_space=pltpu.VMEM)
    hbm = pl.BlockSpec(memory_space=pltpu.HBM)
    dma = pltpu.SemaphoreType.DMA
    table = pl.pallas_call(
        functools.partial(moments_kernel, sections, doms, orders),
        out_shape=jax.ShapeDtypeStruct((2 * bunches + 8, 2 * NBIN), F32),
        in_specs=[hbm] * 9,
        out_specs=vmem,
        scratch_shapes=[
            pltpu.VMEM((bunches, slots), F32),
            pltpu.VMEM((bunches, slots), F32),
            pltpu.VMEM((bunches, slots), jnp.int32),
            pltpu.VMEM((1, bunches), jnp.int32),
            pltpu.VMEM(wake_lags.shape, F32),
            pltpu.VMEM((width, width), F32),
            pltpu.VMEM((1, 2), F32),
            pltpu.VMEM((width, width), F32),
            pltpu.VMEM((width, width), F32),
            pltpu.VMEM((pad + lag_rows, LANES), F32),
            pltpu.VMEM((width, 2 * NBIN), F32),
            pltpu.VMEM((width // 8, slots // 2, LANES), F32),
            pltpu.VMEM((slots // 2, LANES), F32),
            pltpu.VMEM((2, slots // 2, LANES), F32),
            pltpu.VMEM((sections, half // doms, LANES), F32),
            pltpu.VMEM((bunches, width), F32),
            pltpu.VMEM((bunches // 2, 2 * width), F32),
            pltpu.VMEM((own, bunches // 2, 2 * width), F32),
            *[pltpu.VMEM((doms, half // doms, LANES), F32)] * 6,
            dma((10,)),
            dma((sections - 1,)),
            dma((own,)),
            dma((10,)),
        ],
        compiler_params=pltpu.CompilerParams(
            collective_id=0, has_side_effects=True, vmem_limit_bytes=56 * 1024 * 1024
        ),
        name="moments",
    )(
        particles,
        slice_bin,
        bunch_counts.reshape(1, -1),
        past_moments,
        wake_lags,
        wake_matrix,
        adjust_phase.reshape(1, -1),
        *[jnp.asarray(m) for m in plane_maps(orders)],
    )
    return pl.pallas_call(
        track_kernel,
        out_shape=(
            jax.ShapeDtypeStruct(particles.shape, F32),
            jax.ShapeDtypeStruct((bunches, width), F32),
        ),
        in_specs=[vmem, vmem, vmem],
        out_specs=(hbm, hbm),
        scratch_shapes=[pltpu.VMEM(particles.shape, F32), pltpu.VMEM((bunches, width), F32), dma((bunches // 16 + 1,))],
        compiler_params=pltpu.CompilerParams(vmem_limit_bytes=16 * 1024 * 1024),
        name="track",
    )(particles, slice_bin, table)


def solution(mesh):
    in_specs = (
        P(None, "train", "dom"),
        P("train", "dom"),
        P("train"),
        P(None, "train", None),
        P(),
        P(),
        P(),
    )
    out_specs = (P(None, "train", "dom"), P("train", None))
    body = functools.partial(local, mesh.shape["train"], mesh.shape["dom"])
    return jax.shard_map(body, mesh=mesh, in_specs=in_specs, out_specs=out_specs, check_vma=False)
```

```python
import functools

import jax
import jax.numpy as jnp
import numpy as np
from jax import lax
from jax.experimental import pallas as pl
from jax.experimental.pallas import tpu as pltpu
from jax.sharding import PartitionSpec as P

NBIN = 128
LANES = 128
MESH = pl.DeviceIdType.MESH
F32 = jnp.float32
BF16 = jnp.bfloat16


def split(a):
    high = a.astype(BF16)
    return high, (a - high.astype(F32)).astype(BF16)


def dot(a, b):
    return jnp.dot(a, b, preferred_element_type=F32)


def dot3(a_parts, b_parts):
    (ah, al), (bh, bl) = a_parts, b_parts
    return dot(ah, bh) + (dot(ah, bl) + dot(al, bh))


def lane_iota(rows):
    return lax.broadcasted_iota(jnp.int32, (rows, LANES), 1)


def dot_t(a, b):
    return lax.dot_general(a, b, (((1,), (1,)), ((), ())), preferred_element_type=F32)


def dot3_t(a_parts, b_parts):
    (ah, al), (bh, bl) = a_parts, b_parts
    return dot_t(ah, bh) + (dot_t(ah, bl) + dot_t(al, bh))


def merge(a, b, distance, axis):
    low = (lax.broadcasted_iota(jnp.int32, a.shape, axis) & distance) == 0
    return jnp.where(low, a, b) + pltpu.roll(jnp.where(low, b, a), distance, axis)


def product_basis(orders):
    nodes = np.cos((np.arange(orders) + 0.5) * np.pi / orders)
    angle = np.arccos(nodes)
    outer = orders // 8
    products = np.stack(
        [np.cos(8 * a * angle) * np.cos(j * angle) for j in range(8) for a in range(outer)], 1
    )
    legendre = np.polynomial.legendre.legvander(nodes, orders - 1)
    return np.linalg.solve(products, legendre) * (2 * np.arange(orders) + 1)


def plane_maps(orders):
    outer = orders // 8
    one = product_basis(orders)
    both = np.zeros((2 * orders, 2 * orders))
    for c in range(2):
        for j in range(8):
            for a in range(outer):
                row = (j % 2) * orders + ((j // 2) * 2 + c) * outer + a
                both[row, c * orders : (c + 1) * orders] = one[j * outer + a]
    return both.astype(np.float32), np.linalg.inv(both).T.astype(np.float32)


def moments_kernel(
    sections, doms, orders,
    particles, bins, counts, past, lags, wake, phase, to_moments, to_raw,
    out,
    x_buf, y_buf, bin_buf, count_in, lag_in, wake_in, phase_in, to_moments_in, to_raw_in, e_buf, basis_buf,
    stream_buf, twice_buf, poly_buf,
    now_buf, past_in, past_mine, past_buf, dom_buf, conv_buf,
    load_sem, past_send, past_recv, now_send, now_recv, pair_sem,
):
    bunches = counts.shape[1]
    half = orders
    chunks = 4
    width = 2 * orders
    bunches_all = bunches * sections
    own = 2 * sections // doms
    t = lax.axis_index("train")
    d = lax.axis_index("dom")
    dom_send, dom_recv, conv_send, conv_recv = [pair_sem.at[i] for i in range(4)]

    barrier = pltpu.get_barrier_semaphore()
    for o in range(1, sections):
        pl.semaphore_signal(
            barrier, inc=1, device_id=(lax.rem(t + o, sections), d), device_id_type=MESH
        )
    for o in range(1, doms):
        pl.semaphore_signal(
            barrier, inc=1, device_id=(t, lax.rem(d + o, doms)), device_id_type=MESH
        )
    pairs = [
        (counts, count_in),
        (bins, bin_buf),
        (particles.at[0], x_buf),
        (particles.at[2], y_buf),
        (lags, lag_in),
        (wake, wake_in),
        (phase, phase_in),
        (to_moments, to_moments_in),
        (to_raw, to_raw_in),
    ]
    loads = [
        pltpu.make_async_copy(src, dst, load_sem.at[i]) for i, (src, dst) in enumerate(pairs)
    ]
    for copy in loads:
        copy.start()

    late = t // own == d
    owned = jnp.logical_or(late, (sections + t) // own == d)
    turn = jnp.where(late, 1, 0)
    slot = lax.rem(t, own)

    def past_copy(o):
        return pltpu.make_async_remote_copy(
            src_ref=past_mine, dst_ref=past_buf.at[slot],
            send_sem=past_send.at[o - 1], recv_sem=past_recv.at[slot],
            device_id=(lax.rem(t + o, sections), d), device_id_type=MESH,
        )

    def past_here():
        return pltpu.make_async_copy(past.at[turn], past_in, load_sem.at[len(pairs)])

    @pl.when(owned)
    def _():
        past_here().start()

    basis_buf[...] = jnp.zeros_like(basis_buf)
    centers = (lane_iota(1).astype(F32) + 0.5) * (2.0 / NBIN) - 1.0
    previous, current = jnp.ones_like(centers), centers
    for k in range(orders):
        basis_buf[k : k + 1, 0:LANES] = previous
        basis_buf[orders + k : orders + k + 1, LANES : 2 * LANES] = previous
        following = np.float32((2 * k + 3) / (k + 2)) * centers * current
        following = following - np.float32((k + 1) / (k + 2)) * previous
        previous, current = current, following

    pl.semaphore_wait(barrier, sections - 1 + doms - 1)

    @pl.when(owned)
    def _():
        past_here().wait()
        block = past_in[...]
        block = jnp.concatenate([block[: bunches // 2], block[bunches // 2 :]], axis=1)
        past_mine[...] = block
        past_buf[slot] = block
        for o in range(1, sections):
            past_copy(o).start()

    for i in range(1, sections):
        @pl.when(t < i)
        def _():
            now_buf[i] = jnp.zeros(now_buf.shape[1:], F32)

    for copy in loads[0:4]:
        copy.wait()
    slots = x_buf.shape[1]
    deep = slots // 2
    outer = orders // 8
    count = jnp.concatenate([count_in[...], count_in[...]], axis=1)
    slot_index = (
        d * slots
        + jnp.where(lane_iota(LANES) < bunches, 0, deep)
        + lax.broadcasted_iota(jnp.int32, (LANES, LANES), 0)
    )

    def upright(ref, first):
        return jnp.concatenate(
            [ref[:, first : first + LANES], ref[:, deep + first : deep + first + LANES]], axis=0
        ).T

    for first in range(0, deep, LANES):
        here = slice(first, first + LANES)
        z = (upright(bin_buf, first).astype(F32) + 0.5) * (2.0 / NBIN) - 1.0
        twice = z + z
        t2 = twice * z - 1.0
        t4 = 2.0 * t2 * t2 - 1.0
        t8 = 2.0 * t4 * t4 - 1.0
        twice_buf[here, :] = twice
        poly_buf[0, here, :] = jnp.ones_like(z)
        poly_buf[1, here, :] = z
        steps = [None, t8]
        for a in range(2, outer):
            steps.append(2.0 * t8 * steps[a - 1] - (1.0 if a == 2 else steps[a - 2]))
        alive = slot_index + first < count
        for c, ref in enumerate((x_buf, y_buf)):
            v = jnp.where(alive, upright(ref, first), 0.0)
            for a in range(outer):
                stream_buf[c * outer + a, here, :] = v if a == 0 else v * steps[a]

    unroll = 4
    count_f = count.astype(F32)
    for j in range(chunks):

        def rows_step(i, sums):
            sums = list(sums)
            for u in range(unroll):
                here = pl.ds(pl.multiple_of((i * unroll + u) * 8, 8), 8)
                even, odd = poly_buf[0, here, :], poly_buf[1, here, :]
                if j > 0:
                    twice = twice_buf[here, :]
                    even = twice * odd - even
                    odd = twice * even - odd
                    if j < chunks - 1:
                        poly_buf[0, here, :] = even
                        poly_buf[1, here, :] = odd
                for n in range(2 * outer):
                    stream = stream_buf[n, here, :]
                    sums[n] = sums[n] + (stream if j == 0 else stream * even)
                    sums[2 * outer + n] = sums[2 * outer + n] + stream * odd
            return tuple(sums)

        zero = jnp.zeros((8, LANES), F32)
        values = lax.fori_loop(0, deep // (8 * unroll), rows_step, (zero,) * (4 * outer))
        for distance in (1, 2, 4):
            values = [merge(p, q, distance, 0) for p, q in zip(values[::2], values[1::2])]
        moments = merge(values[0], values[1], width, 1) / count_f
        now_buf[t, j] = moments
        dom_buf[d, j] = moments
        for o in range(1, sections):
            @pl.when(t + o < sections)
            def _():
                pltpu.make_async_remote_copy(
                    src_ref=now_buf.at[t, j], dst_ref=now_buf.at[t, j],
                    send_sem=now_send.at[o - 1], recv_sem=now_recv.at[o - 1],
                    device_id=(lax.rem(t + o, sections), d), device_id_type=MESH,
                ).start()

    def now_copy(o):
        return pltpu.make_async_remote_copy(
            src_ref=now_buf.at[t], dst_ref=now_buf.at[t],
            send_sem=now_send.at[o - 1], recv_sem=now_recv.at[o - 1],
            device_id=(lax.rem(t + o, sections), d), device_id_type=MESH,
        )

    def dom_copies(ref, send_sem, recv_sem):
        for o in range(1, doms):
            pltpu.make_async_remote_copy(
                src_ref=ref.at[d], dst_ref=ref.at[d], send_sem=send_sem, recv_sem=recv_sem,
                device_id=(t, lax.rem(d + o, doms)), device_id_type=MESH,
            ).start()

    def whole(ref, send_sem, recv_sem):
        part = ref.at[pl.ds(0, ref.shape[0] - 1)]
        return pltpu.make_async_remote_copy(
            src_ref=part, dst_ref=part, send_sem=send_sem, recv_sem=recv_sem,
            device_id=(t, d), device_id_type=MESH,
        )

    dom_copies(dom_buf, dom_send, dom_recv)

    loads[4].wait()
    rows = bunches_all // 32
    pad = e_buf.shape[0] - rows
    count_lags = lag_in.shape[-1]
    e_buf[...] = jnp.zeros_like(e_buf)
    for row in range(pl.cdiv(count_lags, LANES)):
        size = min(LANES, count_lags - row * LANES)
        e_buf[pad + row : pad + row + 1, 0:size] = lag_in[pl.ds(row * LANES, size)].reshape(1, size)
    plain = e_buf[...]
    lane = lane_iota(plain.shape[0])
    turned = jnp.take_along_axis(plain, LANES - 1 - lane, axis=1, mode="promise_in_bounds")
    moved = pltpu.roll(turned, LANES // 2, 1)
    mixed = jnp.where(lane < LANES // 2, moved, pltpu.roll(moved, 1, 0))
    odd = lax.rem(t, 2)
    e_buf[...] = jnp.where(odd == 1, mixed, turned)
    first_row = pad + rows - 1 - bunches_all // 64 + (t + 1) // 2
    target = lax.broadcasted_iota(jnp.int32, (bunches, LANES), 0)
    source = lane_iota(bunches)

    def toeplitz(tile_first, tiles):
        def rolled(m):
            row = e_buf[pl.ds(first_row - m, 1), :]
            return pltpu.roll(
                jnp.broadcast_to(row, (bunches, LANES)), 0, 1, stride=1, stride_axis=0
            )

        turned_rows = [rolled(tile_first + m) for m in range(-1, tiles)]
        return [
            jnp.where(source >= target, turned_rows[m + 1], turned_rows[m]) for m in range(tiles)
        ]

    low = source < bunches
    above, below = [], []
    for tile in toeplitz(2 * bunches_all // LANES, bunches_all // LANES):
        swapped = pltpu.roll(tile, LANES // 2, 1)
        above += [jnp.where(low, tile, 0.0), jnp.where(low, swapped, 0.0)]
        below += [jnp.where(low, 0.0, swapped), jnp.where(low, 0.0, tile)]
    w_now = split(
        jnp.concatenate([jnp.concatenate(above, axis=1), jnp.concatenate(below, axis=1)], axis=0)
    )
    past_tiles = own * bunches // LANES
    w_past = split(jnp.concatenate(toeplitz(d * past_tiles, past_tiles), axis=1))

    for s in range(own):
        @pl.when(lax.rem(d * own + s, sections) != t)
        def _():
            pltpu.make_async_remote_copy(
                src_ref=past_mine, dst_ref=past_buf.at[s],
                send_sem=past_send.at[0], recv_sem=past_recv.at[s],
                device_id=(t, d), device_id_type=MESH,
            ).wait_recv()

    stored = jnp.concatenate(
        [past_buf[i][:, side * width : (side + 1) * width] for i in range(own) for side in range(2)],
        axis=0,
    )
    for copy in loads[5:]:
        copy.wait()
    raw = dot3_t(split(to_raw_in[...]), split(dot3(w_past, split(stored))))
    convolved = jnp.concatenate([raw[:half], raw[half:]], axis=1)

    for o in range(1, sections):
        @pl.when(o <= t)
        def _():
            now_copy(o).wait_recv()

    gathered = jnp.concatenate(
        [now_buf[i].reshape(half, LANES) for i in range(sections)], axis=1
    )
    conv_buf[d] = convolved + dot3_t(split(gathered), w_now)
    dom_copies(conv_buf, conv_send, conv_recv)

    to_kick = dot3(split(wake_in[...]), split(basis_buf[...]))
    to_kick = dot3(split(to_moments_in[...]), split(to_kick))
    to_kick = split(to_kick[:half]), split(to_kick[half:])
    angle = phase_in[...]
    cosine, sine = jnp.cos(angle), jnp.sin(angle)
    for plane in range(2):
        row = 2 * bunches + 2 * plane
        out[row : row + 1, :] = jnp.broadcast_to(cosine[:, plane : plane + 1], (1, 2 * NBIN))
        out[row + 1 : row + 2, :] = jnp.broadcast_to(sine[:, plane : plane + 1], (1, 2 * NBIN))
    dom_wait = whole(dom_buf, dom_send, dom_recv)
    dom_wait.wait_recv()
    summed = dom_buf[0]
    for i in range(1, doms):
        summed = summed + dom_buf[i]
    def from_packed(packed, maps):
        turned = packed.T
        return dot3(split(turned[:bunches]), maps[0]) + dot3(split(turned[bunches:]), maps[1])

    to_moments_parts = split(to_moments_in[0:half, :]), split(to_moments_in[half:width, :])
    out[bunches : 2 * bunches, 0:width] = from_packed(
        summed.reshape(half, LANES), to_moments_parts
    )

    @pl.when(owned)
    def _():
        for o in range(1, sections):
            past_copy(o).wait_send()

    for o in range(1, sections):
        @pl.when(t + o < sections)
        def _():
            now_copy(o).wait_send()

    dom_wait.wait_send()

    conv_wait = whole(conv_buf, conv_send, conv_recv)
    conv_wait.wait_recv()
    total = conv_buf[0]
    for i in range(1, doms):
        total = total + conv_buf[i]
    out[0:bunches, :] = from_packed(total, to_kick)
    conv_wait.wait_send()


def track_kernel(particles, bins, table, tracked, moments_out, result, moments, sems):
    bunches, slots = bins.shape
    block = 16
    moments[...] = table[bunches : 2 * bunches, 0 : moments.shape[1]]
    through = pltpu.make_async_copy(moments, moments_out, sems.at[bunches // block])
    through.start()
    copies = []
    for i in range(bunches // block):
        rows = slice(i * block, (i + 1) * block)
        for plane in range(2):
            row = 2 * bunches + 2 * plane
            cosine = jnp.broadcast_to(table[row : row + 1, 0:LANES], (block, LANES))
            sine = jnp.broadcast_to(table[row + 1 : row + 2, 0:LANES], (block, LANES))
            kicks = table[rows, plane * NBIN : (plane + 1) * NBIN]
            for first in range(0, slots, LANES):
                here = slice(first, first + LANES)
                place = particles[2 * plane, rows, here]
                momentum = particles[2 * plane + 1, rows, here]
                kick = jnp.take_along_axis(
                    kicks, bins[rows, here], axis=1, mode="promise_in_bounds"
                )
                result[2 * plane, rows, here] = cosine * place + sine * momentum
                result[2 * plane + 1, rows, here] = cosine * momentum - sine * place + kick
        copy = pltpu.make_async_copy(result.at[:, rows, :], tracked.at[:, rows, :], sems.at[i])
        copy.start()
        copies.append(copy)
    for copy in copies:
        copy.wait()
    through.wait()


def local(sections, doms, particles, slice_bin, bunch_counts, past_moments, wake_lags, wake_matrix, adjust_phase):
    _, bunches, slots = particles.shape
    width = wake_matrix.shape[0]
    orders = width // 2
    half = orders
    chunks = 4
    bunches_all = bunches * sections
    own = 2 * sections // doms
    lag_rows = bunches_all // 32
    pad = pl.cdiv(bunches_all // 128, 8) * 8
    vmem = pl.BlockSpec(memory_space=pltpu.VMEM)
    hbm = pl.BlockSpec(memory_space=pltpu.HBM)
    dma = pltpu.SemaphoreType.DMA
    table = pl.pallas_call(
        functools.partial(moments_kernel, sections, doms, orders),
        out_shape=jax.ShapeDtypeStruct((2 * bunches + 8, 2 * NBIN), F32),
        in_specs=[hbm] * 9,
        out_specs=vmem,
        scratch_shapes=[
            pltpu.VMEM((bunches, slots), F32),
            pltpu.VMEM((bunches, slots), F32),
            pltpu.VMEM((bunches, slots), jnp.int32),
            pltpu.VMEM((1, bunches), jnp.int32),
            pltpu.VMEM(wake_lags.shape, F32),
            pltpu.VMEM((width, width), F32),
            pltpu.VMEM((1, 2), F32),
            pltpu.VMEM((width, width), F32),
            pltpu.VMEM((width, width), F32),
            pltpu.VMEM((pad + lag_rows, LANES), F32),
            pltpu.VMEM((width, 2 * NBIN), F32),
            pltpu.VMEM((width // 8, slots // 2, LANES), F32),
            pltpu.VMEM((slots // 2, LANES), F32),
            pltpu.VMEM((2, slots // 2, LANES), F32),
            pltpu.VMEM((sections, chunks, 8, LANES), F32),
            pltpu.VMEM((bunches, width), F32),
            pltpu.VMEM((bunches // 2, 2 * width), F32),
            pltpu.VMEM((own, bunches // 2, 2 * width), F32),
            pltpu.VMEM((doms, chunks, 8, LANES), F32),
            pltpu.VMEM((doms, half, LANES), F32),
            dma((10,)),
            dma((sections - 1,)),
            dma((own,)),
            dma((sections - 1,)),
            dma((sections - 1,)),
            dma((4,)),
        ],
        compiler_params=pltpu.CompilerParams(
            collective_id=0, has_side_effects=True, vmem_limit_bytes=56 * 1024 * 1024
        ),
        name="moments",
    )(
        particles,
        slice_bin,
        bunch_counts.reshape(1, -1),
        past_moments,
        wake_lags,
        wake_matrix,
        adjust_phase.reshape(1, -1),
        *[jnp.asarray(m) for m in plane_maps(orders)],
    )
    return pl.pallas_call(
        track_kernel,
        out_shape=(
            jax.ShapeDtypeStruct(particles.shape, F32),
            jax.ShapeDtypeStruct((bunches, width), F32),
        ),
        in_specs=[vmem, vmem, vmem],
        out_specs=(hbm, hbm),
        scratch_shapes=[pltpu.VMEM(particles.shape, F32), pltpu.VMEM((bunches, width), F32), dma((bunches // 16 + 1,))],
        compiler_params=pltpu.CompilerParams(vmem_limit_bytes=16 * 1024 * 1024),
        name="track",
    )(particles, slice_bin, table)


def solution(mesh):
    in_specs = (
        P(None, "train", "dom"),
        P("train", "dom"),
        P("train"),
        P(None, "train", None),
        P(),
        P(),
        P(),
    )
    out_specs = (P(None, "train", "dom"), P("train", None))
    body = functools.partial(local, mesh.shape["train"], mesh.shape["dom"])
    return jax.shard_map(body, mesh=mesh, in_specs=in_specs, out_specs=out_specs, check_vma=False)
```
